128 devices in a mesh: lat: 16 (over y_lo, z, core), lon: 8 (over y_hi, x).
Axes of the slice: x: 4, y: 4 (y_hi: 2, y_lo: 2; y = y_hi * 2 + y_lo), z: 4, core: 2. Of those that a mesh axis runs over, the one named last changes fastest.
Arguments:
- features: bfloat16 [64, 4096, 256], P('lat', 'lon'), may hold values from -6 to 6
- basis: float32 [64, 9, 25], P('lat'), may hold values from -1.2 to 1.2
- span_lo: int32 [64], P('lat'), may hold values from -2 to 0
- span_hi: int32 [64], P('lat'), may hold values from 0 to 2
- weight: bfloat16 [9, 256, 256], replicated, may hold values from -0.125 to 0.125
- cotangent: bfloat16 [64, 4096, 256], P('lat', 'lon'), may hold values from -6 to 6
Outputs:
- mixed: bfloat16 [64, 4096, 256], P('lat', 'lon')
- grad_input: bfloat16 [64, 4096, 256], P('lat', 'lon')
- grad_weight: float32 [9, 256, 256], replicated
The draws below stay inside these ranges and needn't reach their ends.
All inputs are finite; a program needn't handle non-finite values.
Results may differ from the reference program's by a relative error of at most 0.0049.
Values may be sent and summed in bfloat16 or wider, within the bound.
No kernel may reach another device: no remote copies, remote signals or barrier semaphores. Data moves between devices by JAX's collectives and lax.ppermute only.
A program may use at most 192 MiB of HBM per device.

```python
import math
import jax
import jax.numpy as jnp

C = 256
K = 9
RAD = 2
TAPS = 25
NLAT = 64
NLON = 4096


def touch_ends(entries, own_key, smallest, top_value):
    longest = entries.shape.index(max(entries.shape))
    spots = []
    for shift in (0, 1):
        where = [jax.random.randint(jax.random.fold_in(own_key, axis), (), 0, length) for axis, length in enumerate(entries.shape)]
        where[longest] = (where[longest] + shift) % entries.shape[longest]
        spots.append(tuple(where))
    return entries.at[spots[0]].set(smallest).at[spots[1]].set(top_value)


def levels(key, extent, shards, smallest, largest):
    level = 1.0
    for dim, parts in shards:
        draws = jax.random.uniform(jax.random.fold_in(jax.random.fold_in(key, 6), dim), (parts,), jnp.float32, smallest / len(shards), largest / len(shards))
        level = level * jnp.repeat(jnp.exp(draws), extent[dim] // parts).reshape((-1,) + (1,) * (len(extent) - 1 - dim))
    return level


def normal_values(key, shape, scale, reach, cuts=(), held_as=jnp.bfloat16):
    values = jax.random.normal(key, shape, jnp.float32) * scale
    if len(cuts) > 0:
        values = levels(key, shape, cuts, -0.22, 0.18) * values
    return jnp.clip(values, min=-reach, max=reach).astype(held_as)


def setup_inputs(seed: int = 0) -> dict:
    key_list = jax.random.split(jax.random.key(seed), 7)
    features = normal_values(key_list[0], (NLAT, NLON, C), 1.0, 6.0, ((0, 16), (1, 8)))
    basis = normal_values(key_list[1], (NLAT, K, TAPS), 0.2, 1.2, ((0, 16),), jnp.float32)
    span_lo = touch_ends(jax.random.randint(key_list[2], (NLAT,), -RAD, 1), jax.random.fold_in(key_list[2], 1), -RAD, 0).astype(jnp.int32)
    span_hi = touch_ends(jax.random.randint(key_list[3], (NLAT,), 0, RAD + 1), jax.random.fold_in(key_list[3], 1), 0, RAD).astype(jnp.int32)
    weight = normal_values(key_list[4], (K, C, C), (K * C) ** -0.5, 0.125)
    cotangent = normal_values(key_list[5], (NLAT, NLON, C), 1.0, 6.0, ((0, 16), (1, 8)))
    return dict(features=features, basis=basis, span_lo=span_lo, span_hi=span_hi, weight=weight, cotangent=cotangent)


def kept_basis(basis, span_lo, span_hi):
    offsets = jnp.arange(TAPS, dtype=jnp.int32) // (2 * RAD + 1) - RAD
    keep = (offsets[None, :] >= span_lo[:, None]) & (offsets[None, :] <= span_hi[:, None])
    return jnp.where(keep[:, None, :], basis, jnp.zeros_like(basis))

def reference(features, basis, span_lo, span_hi, weight, cotangent):
    width = 2 * RAD + 1
    kept = kept_basis(basis, span_lo, span_hi)
    padded = jnp.concatenate([features[:, NLON - RAD:], features, features[:, :RAD]], axis=1)
    padded = jnp.pad(padded, ((RAD, RAD), (0, 0), (0, 0)))
    flat_cot = cotangent.reshape(NLAT * NLON, C)
    mixed = jnp.zeros((NLAT * NLON, C), jnp.float32)
    spread = jnp.zeros((NLAT + 2 * RAD, NLON + 2 * RAD, C), jnp.float32)
    grads = []
    for kernel in range(K):
        total = jnp.zeros((NLAT, NLON, C), jnp.float32)
        for tap_index in range(TAPS):
            row_shift = tap_index // width - RAD
            col_shift = tap_index % width - RAD
            window = padded[RAD + row_shift:RAD + row_shift + NLAT, RAD + col_shift:RAD + col_shift + NLON]
            total = total + kept[:, kernel, tap_index][:, None, None] * window.astype(jnp.float32)
        plane = total.astype(jnp.bfloat16).reshape(NLAT * NLON, C)
        mixed = mixed + jnp.dot(plane, weight[kernel], preferred_element_type=jnp.float32)
        grads.append(jnp.dot(plane.T, flat_cot, preferred_element_type=jnp.float32))
        grad_plane = jnp.dot(flat_cot, weight[kernel].T, preferred_element_type=jnp.float32)
        grad_plane = grad_plane.astype(jnp.bfloat16).reshape(NLAT, NLON, C).astype(jnp.float32)
        for tap_index in range(TAPS):
            row_shift = tap_index // width - RAD
            col_shift = tap_index % width - RAD
            spread = spread.at[RAD + row_shift:RAD + row_shift + NLAT, RAD + col_shift:RAD + col_shift + NLON].add(kept[:, kernel, tap_index][:, None, None] * grad_plane)
    middle = spread[RAD:RAD + NLAT]
    grad_input = middle[:, RAD:RAD + NLON]
    grad_input = grad_input.at[:, NLON - RAD:].add(middle[:, :RAD])
    grad_input = grad_input.at[:, :RAD].add(middle[:, NLON + RAD:])
    scale = 1.0 / math.sqrt(NLAT * NLON)
    grad_weight = jnp.stack(grads) * scale
    return (mixed.astype(jnp.bfloat16).reshape(NLAT, NLON, C), grad_input.astype(jnp.bfloat16), grad_weight)
```

```python
import functools
import math

import jax
import jax.numpy as jnp
import numpy as np
from jax import lax
from jax.experimental import pallas as pl
from jax.experimental.pallas import tpu as pltpu
from jax.sharding import Mesh
from jax.sharding import PartitionSpec as P

K = 9
RAD = 2
WIDTH = 2 * RAD + 1
TAPS = WIDTH * WIDTH
ROWS = 4
NJ = 512
C = 256
J = 32
OWN_WINDOW = 64
EXT_WINDOW = 48
LANES = 128
BLOCKS = 2 * K
PADDED_BLOCKS = 20
VMEM = 56 * 1024 * 1024
BF = jnp.bfloat16
F32 = jnp.float32


def kept_basis(basis, span_lo, span_hi):
    offsets = jnp.arange(TAPS, dtype=jnp.int32) // WIDTH - RAD
    keep = (offsets[None, :] >= span_lo[:, None]) & (offsets[None, :] <= span_hi[:, None])
    return jnp.where(keep[:, None, :], basis, jnp.zeros_like(basis))


def band(coef, window, first, depth):
    lane = lax.broadcasted_iota(jnp.int32, (J, depth), 1)
    sub = lax.broadcasted_iota(jnp.int32, (J, depth), 0)
    diff = lane % window - sub - first
    masks = [diff == s for s in range(WIDTH)]

    def build(coef):
        value = jnp.zeros((J, depth), F32)
        for s in range(WIDTH):
            value = jnp.where(masks[s], coef[s : s + 1, :], value)
        return value.astype(BF)

    return build


def own_kernel(coef_ref, cot_ref, feat_ref, z_ref, grad_ref, padded, bands, z_own):
    zero = jnp.zeros((ROWS, 16, C), BF)
    padded[:, 0:16, :] = zero
    padded[:, 16 + NJ : 32 + NJ, :] = zero
    padded[:, 16 : 16 + NJ, :] = cot_ref[...]
    build = band(None, OWN_WINDOW, 16 - RAD, ROWS * OWN_WINDOW)
    for block in range(8 * K):
        bands[block * J : (block + 1) * J, :] = build(coef_ref[block])

    def step(tile, _):
        start = pl.multiple_of(tile * J, J)
        cells = jnp.concatenate([padded[i, pl.ds(start, OWN_WINDOW), :] for i in range(ROWS)], axis=0)
        for row in range(8):
            found = jnp.dot(
                bands[row * K * J : (row + 1) * K * J, :], cells, preferred_element_type=F32
            ).astype(BF)
            for k in range(K):
                piece = found[k * J : (k + 1) * J]
                columns = slice(k * C, (k + 1) * C)
                if 2 <= row < 6:
                    z_own[pl.ds((row - 2) * NJ + start, J), columns] = piece
                else:
                    halo_row = row if row < 2 else row - 4
                    z_ref[pl.ds(halo_row * NJ + start, J), columns] = piece
        return 0

    lax.fori_loop(0, NJ // J, step, 0)
    turned = feat_ref[...].reshape(ROWS * NJ, C).T
    for k in range(K):
        columns = slice(k * C, (k + 1) * C)
        grad_ref[:, columns] = jnp.dot(turned, z_own[:, columns], preferred_element_type=F32)


def own_part(coef, cotangent, features):
    return pl.pallas_call(
        own_kernel,
        out_shape=(
            jax.ShapeDtypeStruct((ROWS * NJ, K * C), BF),
            jax.ShapeDtypeStruct((C, K * C), F32),
        ),
        in_specs=[pl.BlockSpec(memory_space=pltpu.VMEM)] * 3,
        out_specs=[pl.BlockSpec(memory_space=pltpu.VMEM)] * 2,
        scratch_shapes=[
            pltpu.VMEM((ROWS, NJ + 32, C), BF),
            pltpu.VMEM((8 * K * J, ROWS * OWN_WINDOW), BF),
            pltpu.VMEM((ROWS * NJ, K * C), BF),
        ],
        compiler_params=pltpu.CompilerParams(vmem_limit_bytes=VMEM),
        cost_estimate=pl.CostEstimate(
            flops=10_000_000_000, bytes_accessed=15_000_000, transcendentals=0
        ),
        name="own_part",
    )(coef, cotangent, features)


def halo_kernel(core_ref, low_ref, high_ref, z_ref, grad_ref, edge_coef_ref, edge_cot_ref, edge_feat_ref, own_ref, other_ref, total):
    low = low_ref[...].reshape(2 * NJ, C).T
    high = high_ref[...].reshape(2 * NJ, C).T
    turned = jnp.concatenate([low, high], axis=1)
    edge_z = jnp.dot(edge_coef_ref[...], edge_cot_ref[...], preferred_element_type=F32).astype(BF)
    edge_feat = edge_feat_ref[...].T
    for k in range(K):
        columns = slice(k * C, (k + 1) * C)
        total[:, columns] = (
            grad_ref[:, columns]
            + jnp.dot(turned, z_ref[:, columns], preferred_element_type=F32)
            + jnp.dot(edge_feat, edge_z[k * 32 : (k + 1) * 32], preferred_element_type=F32)
        )
    core = core_ref[0]
    mine = pl.multiple_of(core * LANES, LANES)
    theirs = pl.multiple_of((1 - core) * LANES, LANES)
    for block in range(BLOCKS):
        columns = slice(block * LANES, (block + 1) * LANES)
        own_ref[block] = total[pl.ds(mine, LANES), columns]
        other_ref[block] = total[pl.ds(theirs, LANES), columns].astype(BF)
    for block in range(BLOCKS, PADDED_BLOCKS):
        own_ref[block] = jnp.zeros((LANES, LANES), F32)
        other_ref[block] = jnp.zeros((LANES, LANES), BF)


def halo_part(core, low, high, z, grad, edge_coef, edge_cot, edge_feat):
    shape = (PADDED_BLOCKS, LANES, LANES)
    return pl.pallas_call(
        halo_kernel,
        out_shape=(jax.ShapeDtypeStruct(shape, F32), jax.ShapeDtypeStruct(shape, BF)),
        in_specs=[pl.BlockSpec(memory_space=pltpu.SMEM)] + [pl.BlockSpec(memory_space=pltpu.VMEM)] * 7,
        out_specs=[pl.BlockSpec(memory_space=pltpu.VMEM)] * 2,
        scratch_shapes=[pltpu.VMEM((C, K * C), F32)],
        compiler_params=pltpu.CompilerParams(vmem_limit_bytes=VMEM),
        cost_estimate=pl.CostEstimate(
            flops=2_400_000_000, bytes_accessed=15_000_000, transcendentals=0
        ),
        name="halo_part",
    )(core, low, high, z, grad, edge_coef, edge_cot, edge_feat)


def mix_kernel(coef_ref, ext_ref, weight_ref, _, out_ref, bands, filtered):
    depth = WIDTH * EXT_WINDOW
    build = band(None, EXT_WINDOW, 8 - RAD, depth)
    row = pl.program_id(0)
    for k in range(K):
        bands[k * J : (k + 1) * J, :] = build(coef_ref[0, k])

    def step(tile, _):
        start = pl.multiple_of(tile * J, J)
        cells = jnp.concatenate(
            [ext_ref[row + r, pl.ds(start, EXT_WINDOW), :] for r in range(WIDTH)], axis=0
        )
        found = jnp.dot(bands[...], cells, preferred_element_type=F32).astype(BF)
        for k in range(K):
            filtered[pl.ds(start, J), k * C : (k + 1) * C] = found[k * J : (k + 1) * J]
        return 0

    lax.fori_loop(0, NJ // J, step, 0, unroll=4)
    out_ref[0] = jnp.dot(filtered[...], weight_ref[...], preferred_element_type=F32).astype(BF)


def mix_part(coef, extended, weight, after, name):
    return pl.pallas_call(
        mix_kernel,
        grid=(ROWS,),
        out_shape=jax.ShapeDtypeStruct((ROWS, NJ, C), BF),
        in_specs=[
            pl.BlockSpec((1, K, WIDTH, WIDTH * EXT_WINDOW), lambda i: (i, 0, 0, 0)),
            pl.BlockSpec(memory_space=pltpu.VMEM),
            pl.BlockSpec(memory_space=pltpu.VMEM),
            pl.BlockSpec(memory_space=pl.ANY),
        ],
        out_specs=pl.BlockSpec((1, NJ, C), lambda i: (i, 0, 0)),
        scratch_shapes=[
            pltpu.VMEM((K * J, WIDTH * EXT_WINDOW), BF),
            pltpu.VMEM((NJ, K * C), BF),
        ],
        compiler_params=pltpu.CompilerParams(vmem_limit_bytes=VMEM),
        cost_estimate=pl.CostEstimate(
            flops=10_000_000_000, bytes_accessed=5_000_000, transcendentals=0
        ),
        name=name,
    )(coef, extended, weight, after)


def edge_choice():
    choice = np.zeros((TAPS, ROWS, 8, 4, 4), np.float32)
    halo_columns = (-2, -1, NJ, NJ + 1)
    edge_columns = (0, 1, NJ - 2, NJ - 1)
    for i in range(ROWS):
        for place in range(8):
            d = place - RAD - i
            for a, target in enumerate(edge_columns):
                for b, source in enumerate(halo_columns):
                    e = target - source
                    if abs(d) <= RAD and abs(e) <= RAD:
                        choice[(d + RAD) * WIDTH + e + RAD, i, place, a, b] = 1.0
    return choice


def shifted(block, axis, count, step, periodic):
    route = [(i, (i + step) % count) for i in range(count) if periodic or 0 <= i + step < count]
    return lax.ppermute(block, axis, route)


def per_device(features, basis, span_lo, span_hi, weight, cotangent):
    lat = ("yz", "core")
    lats, lons = lax.axis_size("yz") * lax.axis_size("core"), lax.axis_size("lon")
    core = lax.axis_index("core")
    kept = kept_basis(basis, span_lo, span_hi)

    low = shifted(features[ROWS - 2 :], lat, lats, 1, False)
    high = shifted(features[:2], lat, lats, -1, False)
    left = shifted(cotangent[:, NJ - 2 :], "lon", lons, 1, True)
    right = shifted(cotangent[:, :2], "lon", lons, -1, True)

    cells = kept.reshape(ROWS, K, WIDTH, WIDTH)[..., ::-1]
    spread = jnp.stack([jnp.pad(cells[i], ((0, 0), (i, 3 - i), (0, 0))) for i in range(ROWS)])
    own_coef = jnp.transpose(spread, (2, 1, 3, 0)).reshape(8 * K, WIDTH, ROWS)
    own_coef = jnp.repeat(own_coef, OWN_WINDOW, axis=2)
    z, grad_own = own_part(own_coef, cotangent, features)

    edge_coef = jnp.einsum("ikt,tipab->kpaib", kept, edge_choice()).reshape(K * 32, ROWS * 4).astype(BF)
    edge_coef = jnp.pad(edge_coef, ((0, 0), (0, LANES - ROWS * 4)))
    edge_cot = jnp.concatenate([left, right], axis=1).reshape(ROWS * 4, C)
    edge_cot = jnp.pad(edge_cot, ((0, LANES - ROWS * 4), (0, 0)))
    rows = jnp.concatenate([low, features, high], axis=0)
    edge_feat = jnp.concatenate([rows[:, :2], rows[:, NJ - 2 :]], axis=1).reshape(32, C)
    own, other = halo_part(
        core.reshape(1).astype(jnp.int32), low, high, z, grad_own, edge_coef, edge_cot, edge_feat
    )

    swap = [(0, 1), (1, 0)]
    chips = ("yz", "lon")
    parts = lax.axis_size("yz") * lons
    half = own + lax.ppermute(other, "core", swap).astype(F32)
    pieces = half.astype(BF).reshape(parts, PADDED_BLOCKS * LANES // parts, LANES)
    pieces = lax.all_to_all(pieces, chips, 0, 0)
    scale = 1.0 / math.sqrt(ROWS * lats * NJ * lons)
    piece = (jnp.sum(pieces.astype(F32), axis=0) * scale).astype(BF)
    gathered = lax.all_to_all(jnp.broadcast_to(piece, pieces.shape), chips, 0, 0)
    gathered = gathered.reshape(PADDED_BLOCKS, LANES, LANES)[:BLOCKS]
    swapped = lax.ppermute(gathered, "core", swap)
    first = jnp.where(core == 0, gathered, swapped)
    second = jnp.where(core == 0, swapped, gathered)
    halves = jnp.stack([first, second]).reshape(2, K, 2, LANES, LANES)
    grad_weight = jnp.transpose(halves, (1, 0, 3, 2, 4)).reshape(K, C, C).astype(F32)

    edges = shifted(rows[:, NJ - 2 :], "lon", lons, 1, True), shifted(rows[:, :2], "lon", lons, -1, True)
    gap = jnp.zeros((8, 6, C), BF)
    feat_ext = jnp.concatenate([gap, edges[0], rows, edges[1], gap], axis=1)
    feat_coef = kept.reshape(ROWS, K, WIDTH, WIDTH).transpose(0, 1, 3, 2)
    feat_coef = jnp.repeat(feat_coef, EXT_WINDOW, axis=3)
    mixed = mix_part(feat_coef, feat_ext, weight.reshape(K * C, C), own, "mixed_part")

    wide = jnp.concatenate([gap[:ROWS], left, cotangent, right, gap[:ROWS]], axis=1)
    cot_low = shifted(wide[ROWS - 2 :], lat, lats, 1, False)
    cot_high = shifted(wide[:2], lat, lats, -1, False)
    cot_ext = jnp.concatenate([cot_low, wide, cot_high], axis=0)
    kept_low = shifted(kept[ROWS - 2 :], lat, lats, 1, False)
    kept_high = shifted(kept[:2], lat, lats, -1, False)
    kept_ext = jnp.concatenate([kept_low, kept, kept_high], axis=0)
    flipped = kept_ext[..., ::-1].reshape(8, K, WIDTH, WIDTH)
    cot_coef = jnp.stack(
        [jnp.stack([flipped[i + r, :, r] for r in range(WIDTH)], axis=-1) for i in range(ROWS)]
    )
    cot_coef = jnp.repeat(cot_coef, EXT_WINDOW, axis=3)
    turned = jnp.transpose(weight, (0, 2, 1)).reshape(K * C, C)
    grad_input = mix_part(cot_coef, cot_ext, turned, own, "grad_input_part")
    return mixed, grad_input, grad_weight


def solution(mesh):
    lats, lons = mesh.devices.shape
    split = Mesh(mesh.devices.reshape(lats // 2, 2, lons), ("yz", "core", "lon"))
    lat = ("yz", "core")
    return jax.shard_map(
        per_device,
        mesh=split,
        in_specs=(P(lat, "lon", None), P(lat, None, None), P(lat), P(lat), P(), P(lat, "lon", None)),
        out_specs=(P(lat, "lon", None), P(lat, "lon", None), P()),
        check_vma=False,
    )
```

```python
import functools
import math

import jax
import jax.numpy as jnp
from jax import lax
from jax.experimental import pallas as pl
from jax.experimental.pallas import tpu as pltpu
from jax.sharding import Mesh
from jax.sharding import PartitionSpec as P

K = 9
RAD = 2
WIDTH = 2 * RAD + 1
TAPS = WIDTH * WIDTH
ROWS = 4
PLACES = ROWS + 2 * RAD
NJ = 512
C = 256
J = 32
STEPS = NJ // J
EDGE = 16
OWN_WINDOW = 64
EXT_WINDOW = 48
EXT = NJ + 16
LANES = 128
BLOCKS = 2 * K
PADDED_BLOCKS = 20
MIB = 1024 * 1024
BF = jnp.bfloat16
F32 = jnp.float32

IN_VMEM = pl.BlockSpec(memory_space=pltpu.VMEM)
IN_SMEM = pl.BlockSpec(memory_space=pltpu.SMEM)
IN_HBM = pl.BlockSpec(memory_space=pltpu.HBM)
ANYWHERE = pl.BlockSpec(memory_space=pl.ANY)


def in_hbm(array):
    return pltpu.with_memory_space_constraint(array, pltpu.HBM)


def params(mib):
    return pltpu.CompilerParams(vmem_limit_bytes=mib * MIB)


def cost(flops, moved):
    return pl.CostEstimate(flops=int(flops), bytes_accessed=int(moved), transcendentals=0)


def banded(line):
    return pltpu.roll(jnp.broadcast_to(line, (J, 256)), 0, axis=1, stride=1, stride_axis=0).astype(BF)


def one_hot(lane_of_tap):
    tap = lax.broadcasted_iota(jnp.int32, (LANES, 256), 0)
    lane = lax.broadcasted_iota(jnp.int32, (LANES, 256), 1)
    return jnp.where((lane == lane_of_tap(tap)) & (tap < TAPS), 1.0, 0.0).astype(BF)


def send_kernel(lo_ref, hi_ref, basis_ref, feat_ref, cot_ref, chip_ref, link_ref, kept_ref, lines_ref, lo, hi, sems):
    core = lax.axis_index("core")
    to_chip, to_link = 2 - 2 * core, 2 * core
    copies = [
        (lo_ref, lo),
        (hi_ref, hi),
        (feat_ref.at[pl.ds(to_link, 2)], link_ref.at[pl.ds(0, 2), pl.ds(0, NJ)]),
        (cot_ref.at[pl.ds(to_link, 2)], link_ref.at[pl.ds(2, 2), pl.ds(0, NJ)]),
        (feat_ref.at[pl.ds(to_chip, 2)], chip_ref.at[pl.ds(0, 2), pl.ds(0, NJ)]),
        (cot_ref.at[pl.ds(to_chip, 2)], chip_ref.at[pl.ds(2, 2), pl.ds(0, NJ)]),
    ]
    copies = [pltpu.make_async_copy(a, b, sems.at[n]) for n, (a, b) in enumerate(copies)]
    for copy in copies:
        copy.start()
    offset = lax.broadcasted_iota(jnp.int32, (16, LANES), 1) // WIDTH - RAD
    for ref in (chip_ref, link_ref):
        ref[:, NJ:, :] = jnp.zeros((ROWS, 16, C), BF)
    copies[0].wait()
    copies[1].wait()
    lines = jnp.zeros((16, 256), F32)
    for i in range(ROWS):
        cells = jnp.pad(basis_ref[:, i, :], ((0, 16 - K), (0, LANES - TAPS)))
        cells = jnp.where((offset >= lo[i]) & (offset <= hi[i]), cells, jnp.zeros_like(cells)).astype(BF)
        kept_ref[i] = cells
        place = one_hot(lambda tap, i=i: i * OWN_WINDOW + (TAPS - 1 - tap) - WIDTH * i + 16)
        lines = lines + jnp.dot(cells, place, preferred_element_type=F32)
    lines_ref[...] = lines
    for n in range(2):
        link_ref[2 + n, NJ:, 0:LANES] = kept_ref[to_link + n]
        chip_ref[2 + n, NJ:, 0:LANES] = kept_ref[to_chip + n]
    for copy in copies[2:]:
        copy.wait()


def send_part(span_lo, span_hi, basis, features, cotangent):
    return pl.pallas_call(
        send_kernel,
        out_shape=(
            pltpu.VMEM((ROWS, EXT, C), BF),
            pltpu.VMEM((ROWS, EXT, C), BF),
            pltpu.VMEM((ROWS, 16, LANES), BF),
            pltpu.VMEM((16, 256), F32),
        ),
        in_specs=[IN_HBM, IN_HBM, IN_VMEM, IN_HBM, IN_HBM],
        out_specs=[IN_VMEM] * 4,
        scratch_shapes=[
            pltpu.SMEM((ROWS,), jnp.int32),
            pltpu.SMEM((ROWS,), jnp.int32),
            pltpu.SemaphoreType.DMA((6,)),
        ],
        compiler_params=params(8),
        cost_estimate=cost(0, 4e6),
        name="send_part",
    )(in_hbm(span_lo), in_hbm(span_hi), jnp.transpose(basis, (1, 0, 2)), in_hbm(features), in_hbm(cotangent))


def own_kernel(lines_ref, cot_ref, feat_ref, z_ref, grad_ref, bands_ref, to_right_ref, to_left_ref, padded, z_own):
    zero = jnp.zeros((ROWS, EDGE, C), BF)
    padded[:, 0:EDGE, :] = zero
    padded[:, EDGE + NJ :, :] = zero
    padded[:, EDGE : EDGE + NJ, :] = cot_ref[...]
    to_right_ref[...] = cot_ref[:, NJ - EDGE :, :]
    to_left_ref[...] = cot_ref[:, :EDGE, :]
    window_cell = lax.broadcasted_iota(jnp.int32, (16, 256), 1) % OWN_WINDOW
    inside = (window_cell >= EDGE - RAD) & (window_cell <= EDGE + RAD)
    for place in range(PLACES):
        lines = pltpu.roll(lines_ref[...], (WIDTH * place - 22) % 256, axis=1)
        lines = jnp.where(inside, lines, jnp.zeros_like(lines))
        for k in range(K):
            block = place * K + k
            bands_ref[block * J : (block + 1) * J, :] = banded(lines[k : k + 1, :])

    def step(tile, _):
        start = pl.multiple_of(tile * J, J)
        cells = jnp.concatenate([padded[i, pl.ds(start, OWN_WINDOW), :] for i in range(ROWS)], axis=0)
        for place in range(PLACES):
            found = jnp.dot(
                bands_ref[place * K * J : (place + 1) * K * J, :], cells, preferred_element_type=F32
            ).astype(BF)
            for k in range(K):
                piece = found[k * J : (k + 1) * J]
                columns = slice(k * C, (k + 1) * C)
                if 2 <= place < 6:
                    z_own[pl.ds((place - 2) * NJ + start, J), columns] = piece
                else:
                    halo = place if place < 2 else place - 4
                    z_ref[pl.ds(halo * NJ + start, J), columns] = piece
        return 0

    lax.fori_loop(0, STEPS, step, 0, unroll=4)
    turned = feat_ref[...].reshape(ROWS * NJ, C).T
    for k in range(K):
        columns = slice(k * C, (k + 1) * C)
        grad_ref[:, columns] = jnp.dot(turned, z_own[:, columns], preferred_element_type=F32)


def own_part(lines, cotangent, features):
    return pl.pallas_call(
        own_kernel,
        out_shape=(
            pltpu.VMEM((ROWS * NJ, K * C), BF),
            pltpu.VMEM((C, K * C), F32),
            pltpu.VMEM((PLACES * K * J, 256), BF),
            pltpu.VMEM((ROWS, EDGE, C), BF),
            pltpu.VMEM((ROWS, EDGE, C), BF),
        ),
        in_specs=[IN_VMEM] * 3,
        out_specs=[IN_VMEM] * 5,
        scratch_shapes=[
            pltpu.VMEM((ROWS, NJ + 2 * EDGE, C), BF),
            pltpu.VMEM((ROWS * NJ, K * C), BF),
        ],
        compiler_params=params(18),
        cost_estimate=cost(10e9, 4e6),
        name="own_part",
    )(lines, cotangent, features)


def halo_kernel(
    chip_ref, link_ref, left_ref, right_ref, feat_ref, z_ref, grad_ref, bands_ref,
    own_ref, other_ref, to_right_ref, to_left_ref, total, edge_z,
):
    core = lax.axis_index("core")
    from_chip = chip_ref[0:2, 0:NJ, :].reshape(2 * NJ, C).T
    from_link = link_ref[0:2, 0:NJ, :].reshape(2 * NJ, C).T
    chip_rows = pl.ds(pl.multiple_of((1 - core) * 2 * NJ, 2 * NJ), 2 * NJ)
    link_rows = pl.ds(pl.multiple_of(core * 2 * NJ, 2 * NJ), 2 * NJ)
    gap = jnp.zeros((OWN_WINDOW - 2 * EDGE, C), BF)
    pieces = []
    for i in range(ROWS):
        pieces += [left_ref[i], gap, right_ref[i]]
    cells = jnp.concatenate(pieces, axis=0)
    for place in range(PLACES):
        found = jnp.dot(
            bands_ref[place * K * J : (place + 1) * K * J, :], cells, preferred_element_type=F32
        ).astype(BF)
        for k in range(K):
            edge_z[place * J : (place + 1) * J, k * C : (k + 1) * C] = found[k * J : (k + 1) * J]
    first, last = slice(0, EDGE), slice(NJ - EDGE, NJ)

    def ends(n):
        chip = [chip_ref[n, part, :] for part in (first, last)]
        link = [link_ref[n, part, :] for part in (first, last)]
        low = [jnp.where(core == 0, b, a) for a, b in zip(chip, link, strict=True)]
        high = [jnp.where(core == 0, a, b) for a, b in zip(chip, link, strict=True)]
        return low, high

    halo = [ends(n) for n in range(4)]
    rows = [halo[0][0], halo[1][0]]
    rows += [[feat_ref[i, part, :] for part in (first, last)] for i in range(ROWS)]
    rows += [halo[0][1], halo[1][1]]
    edge_feat = jnp.concatenate([end for row in rows for end in row], axis=0).T
    for n, row in enumerate(rows + [halo[2][0], halo[3][0], halo[2][1], halo[3][1]]):
        to_left_ref[n], to_right_ref[n] = row
    for k in range(K):
        columns = slice(k * C, (k + 1) * C)
        total[:, columns] = (
            grad_ref[:, columns]
            + jnp.dot(from_chip, z_ref[chip_rows, columns], preferred_element_type=F32)
            + jnp.dot(from_link, z_ref[link_rows, columns], preferred_element_type=F32)
            + jnp.dot(edge_feat, edge_z[:, columns], preferred_element_type=F32)
        )
    mine = pl.multiple_of(core * LANES, LANES)
    theirs = pl.multiple_of((1 - core) * LANES, LANES)
    for block in range(BLOCKS):
        columns = slice(block * LANES, (block + 1) * LANES)
        own_ref[block] = total[pl.ds(mine, LANES), columns]
        other_ref[block] = total[pl.ds(theirs, LANES), columns].astype(BF)
    for block in range(BLOCKS, PADDED_BLOCKS):
        own_ref[block] = jnp.zeros((LANES, LANES), F32)
        other_ref[block] = jnp.zeros((LANES, LANES), BF)


def halo_part(chip, link, left, right, features, z, grad, bands):
    shape = (PADDED_BLOCKS, LANES, LANES)
    return pl.pallas_call(
        halo_kernel,
        out_shape=(
            pltpu.VMEM(shape, F32),
            pltpu.VMEM(shape, BF),
            pltpu.VMEM((12, EDGE, C), BF),
            pltpu.VMEM((12, EDGE, C), BF),
        ),
        in_specs=[IN_VMEM] * 8,
        out_specs=[IN_VMEM] * 4,
        scratch_shapes=[pltpu.VMEM((C, K * C), F32), pltpu.VMEM((PLACES * J, K * C), BF)],
        compiler_params=params(14),
        cost_estimate=cost(4e9, 4e6),
        name="halo_part",
    )(chip, link, left, right, features, z, grad, bands)


def half_kernel(own_ref, other_ref, to_right_in, to_left_in, out_ref, to_right_ref, to_left_ref):
    out_ref[...] = (own_ref[...] + other_ref[...].astype(F32)).astype(BF)
    to_right_ref[...] = to_right_in[...]
    to_left_ref[...] = to_left_in[...]


def half_part(own, other, to_right, to_left):
    return pl.pallas_call(
        half_kernel,
        out_shape=(
            pltpu.VMEM(own.shape, BF),
            pltpu.VMEM(to_right.shape, BF),
            pltpu.VMEM(to_left.shape, BF),
        ),
        in_specs=[IN_VMEM] * 4,
        out_specs=[IN_VMEM] * 3,
        compiler_params=params(4),
        cost_estimate=cost(1e6, 3e6),
        name="half_part",
    )(own, other, to_right, to_left)


def sum_kernel(scale, pieces_ref, _, out_ref):
    piece = (jnp.sum(pieces_ref[...].astype(F32), axis=0) * scale).astype(BF)
    out_ref[...] = jnp.broadcast_to(piece, out_ref.shape)


def sum_part(pieces, scale, after):
    return pl.pallas_call(
        functools.partial(sum_kernel, scale),
        out_shape=pltpu.VMEM(pieces.shape, BF),
        in_specs=[IN_VMEM, ANYWHERE],
        out_specs=IN_VMEM,
        compiler_params=params(4),
        cost_estimate=cost(1e6, 2e6),
        name="sum_part",
    )(pieces, after)


def order_kernel(*_):
    pass


def ordered(value, after):
    return pl.pallas_call(
        order_kernel,
        out_shape=jax.ShapeDtypeStruct(value.shape, value.dtype),
        in_specs=[ANYWHERE, ANYWHERE],
        out_specs=ANYWHERE,
        input_output_aliases={0: 0},
        compiler_params=params(1),
        name="ordered",
    )(value, after)


def result_kernel(own_ref, other_ref, out_ref):
    core = lax.axis_index("core")
    for n in range(out_ref.shape[0]):
        for part in range(2):
            columns = slice(part * LANES, (part + 1) * LANES)
            mine = own_ref[2 * n + part].astype(F32)
            theirs = other_ref[2 * n + part].astype(F32)
            out_ref[n, pl.ds(pl.multiple_of(core * LANES, LANES), LANES), columns] = mine
            out_ref[n, pl.ds(pl.multiple_of((1 - core) * LANES, LANES), LANES), columns] = theirs


def result_part(own, other):
    step = 3
    return pl.pallas_call(
        result_kernel,
        grid=(K // step,),
        out_shape=jax.ShapeDtypeStruct((K, C, C), F32),
        in_specs=[pl.BlockSpec((2 * step, LANES, LANES), lambda n: (n, 0, 0))] * 2,
        out_specs=pl.BlockSpec((step, C, C), lambda n: (n, 0, 0)),
        compiler_params=params(6),
        cost_estimate=cost(1e6, 4e6),
        name="result_part",
    )(own, other)


def mix_rows(lines, extended, weight_copy, weight, out_ref, bands, filtered, mixed, sems, turned=None):
    copies = [pltpu.make_async_copy(mixed.at[row], out_ref.at[row], sems.at[row]) for row in range(ROWS)]
    for row in range(ROWS):
        slot = row % 2
        for k in range(K):
            bands[slot, k * J : (k + 1) * J, :] = banded(lines[row][k : k + 1, :])[:, : WIDTH * EXT_WINDOW]
        for tile in range(STEPS):
            start = tile * J
            cells = jnp.concatenate(
                [extended[row + r, start : start + EXT_WINDOW, :] for r in range(WIDTH)], axis=0
            )
            found = jnp.dot(bands[slot], cells, preferred_element_type=F32).astype(BF)
            for k in range(K):
                filtered[slot, start : start + J, k * C : (k + 1) * C] = found[k * J : (k + 1) * J]
        if row == 0:
            weight_copy.wait()
            if turned is not None:
                for k in range(K):
                    turned[k * C : (k + 1) * C, :] = weight[k].T
                weight = turned
        mixed[row] = jnp.dot(filtered[slot], weight[...], preferred_element_type=F32).astype(BF)
        copies[row].start()
    for copy in copies:
        copy.wait()


def extend(extended, n, row, left, right):
    extended[n] = jnp.concatenate([left[8:], row, right[:8]], axis=0)


def mixed_kernel(kept_ref, chip_ref, link_ref, left_ref, right_ref, feat_hbm, weight_hbm, _, out_ref, done_ref, feat, weight, extended, bands, filtered, mixed, sems):
    core = lax.axis_index("core")
    feat_copy = pltpu.make_async_copy(feat_hbm, feat, sems.at[ROWS])
    weight_copy = pltpu.make_async_copy(weight_hbm, weight, sems.at[ROWS + 1])
    feat_copy.start()
    weight_copy.start()

    def fill(low, high):
        for n in range(2):
            extend(extended, n, low[n, 0:NJ, :], left_ref[n], right_ref[n])
            extend(extended, 6 + n, high[n, 0:NJ, :], left_ref[6 + n], right_ref[6 + n])

    pl.when(core == 0)(lambda: fill(link_ref, chip_ref))
    pl.when(core == 1)(lambda: fill(chip_ref, link_ref))
    place = one_hot(lambda tap: tap // WIDTH * EXT_WINDOW + 8 - RAD + tap % WIDTH)
    lines = [jnp.dot(kept_ref[row], place, preferred_element_type=F32) for row in range(ROWS)]
    feat_copy.wait()
    for n in range(ROWS):
        extend(extended, 2 + n, feat[n], left_ref[2 + n], right_ref[2 + n])
    mix_rows(lines, extended, weight_copy, weight, out_ref, bands, filtered, mixed, sems)
    done_ref[...] = jnp.zeros_like(done_ref)


def grad_kernel(kept_ref, chip_ref, link_ref, near_left_ref, near_right_ref, left_ref, right_ref, cot_hbm, weight_hbm, _, out_ref, done_ref, cot, weight, extended, bands, filtered, mixed, sems, cells, turned):
    core = lax.axis_index("core")
    cot_copy = pltpu.make_async_copy(cot_hbm, cot, sems.at[ROWS])
    weight_copy = pltpu.make_async_copy(weight_hbm, weight, sems.at[ROWS + 1])
    cot_copy.start()
    weight_copy.start()

    def fill(low, high):
        for n in range(2):
            extend(extended, n, low[2 + n, 0:NJ, :], left_ref[PLACES + n], right_ref[PLACES + n])
            extend(extended, 6 + n, high[2 + n, 0:NJ, :], left_ref[PLACES + 2 + n], right_ref[PLACES + 2 + n])
            cells[n] = low[2 + n, NJ:, 0:LANES]
            cells[6 + n] = high[2 + n, NJ:, 0:LANES]

    pl.when(core == 0)(lambda: fill(link_ref, chip_ref))
    pl.when(core == 1)(lambda: fill(chip_ref, link_ref))
    for n in range(ROWS):
        cells[2 + n] = kept_ref[n]

    away = (TAPS - 1 - lax.broadcasted_iota(jnp.int32, (16, LANES), 1)) // WIDTH
    place = one_hot(lambda tap: (TAPS - 1 - tap) // WIDTH * EXT_WINDOW + 8 - RAD + (TAPS - 1 - tap) % WIDTH)
    lines = []
    for row in range(ROWS):
        taken = jnp.zeros((16, LANES), F32)
        for r in range(WIDTH):
            taken = jnp.where(away == r, cells[row + r].astype(F32), taken)
        lines.append(jnp.dot(taken.astype(BF), place, preferred_element_type=F32))
    cot_copy.wait()
    for n in range(ROWS):
        extend(extended, 2 + n, cot[n], near_left_ref[n], near_right_ref[n])
    mix_rows(lines, extended, weight_copy, weight, out_ref, bands, filtered, mixed, sems, turned)
    done_ref[...] = jnp.zeros_like(done_ref)


def mix_part(kernel, operands, field, weight, after, extra, name):
    return pl.pallas_call(
        kernel,
        out_shape=(jax.ShapeDtypeStruct((ROWS, NJ, C), BF), pltpu.VMEM((8, LANES), F32)),
        in_specs=[IN_VMEM] * len(operands) + [IN_HBM, IN_HBM, ANYWHERE],
        out_specs=[IN_HBM, IN_VMEM],
        scratch_shapes=[
            pltpu.VMEM(field.shape, BF),
            pltpu.VMEM(weight.shape, BF),
            pltpu.VMEM((PLACES, EXT, C), BF),
            pltpu.VMEM((2, K * J, WIDTH * EXT_WINDOW), BF),
            pltpu.VMEM((2, NJ, K * C), BF),
            pltpu.VMEM((ROWS, NJ, C), BF),
            pltpu.SemaphoreType.DMA((ROWS + 2,)),
        ]
        + extra,
        compiler_params=params(20),
        cost_estimate=cost(8e9, 5e6),
        name=name,
    )(*operands, in_hbm(field), in_hbm(weight), after)


def shifted(block, axis, count, step, periodic):
    route = [(i, (i + step) % count) for i in range(count) if periodic or 0 <= i + step < count]
    return lax.ppermute(block, axis, route)


def per_device(features, basis, span_lo, span_hi, weight, cotangent):
    lat, chips = ("yz", "core"), ("yz", "lon")
    lats, lons = lax.axis_size("yz") * lax.axis_size("core"), lax.axis_size("lon")
    parts = lax.axis_size("yz") * lons
    swap = [(0, 1), (1, 0)]

    chip, link, kept, lines = send_part(span_lo, span_hi, basis, features, cotangent)
    pairs = [(i, i + 1) for i in range(1, lats - 1, 2)]
    link = lax.ppermute(link, lat, pairs + [(b, a) for a, b in pairs])
    chip = lax.ppermute(chip, "core", swap)

    z, grad_own, bands, to_right, to_left = own_part(lines, cotangent, features)
    near_left = shifted(to_right, "lon", lons, 1, True)
    near_right = shifted(to_left, "lon", lons, -1, True)
    own, other, to_right, to_left = halo_part(
        chip, link, near_left, near_right, features, z, grad_own, bands
    )

    half, to_right, to_left = half_part(own, lax.ppermute(other, "core", swap), to_right, to_left)
    pieces = lax.all_to_all(half.reshape(parts, -1, LANES), chips, 0, 0)
    left = shifted(to_right, "lon", lons, 1, True)
    right = shifted(to_left, "lon", lons, -1, True)
    mixed, mixed_done = mix_part(
        mixed_kernel, (kept, chip, link, left, right), features, weight.reshape(K * C, C), half, [],
        "mixed_part",
    )
    scale = 1.0 / math.sqrt(ROWS * lats * NJ * lons)
    copies = sum_part(pieces, scale, mixed_done)
    gathered = lax.all_to_all(copies, chips, 0, 0).reshape(PADDED_BLOCKS, LANES, LANES)
    grad_input, grad_done = mix_part(
        grad_kernel,
        (kept, chip, link, near_left, near_right, left, right),
        cotangent, weight, copies,
        [pltpu.VMEM((PLACES, 16, LANES), BF), pltpu.VMEM((K * C, C), BF)],
        "grad_input_part",
    )
    gathered = ordered(gathered, grad_done)
    grad_weight = result_part(gathered, lax.ppermute(gathered, "core", swap))
    return mixed, grad_input, grad_weight


def solution(mesh):
    lats, lons = mesh.devices.shape
    split = Mesh(mesh.devices.reshape(lats // 2, 2, lons), ("yz", "core", "lon"))
    lat = ("yz", "core")
    return jax.shard_map(
        per_device,
        mesh=split,
        in_specs=(P(lat, "lon", None), P(lat, None, None), P(lat), P(lat), P(), P(lat, "lon", None)),
        out_specs=(P(lat, "lon", None), P(lat, "lon", None), P()),
        check_vma=False,
    )
```

```python
import functools
import math

import jax
import jax.numpy as jnp
from jax import lax
from jax.experimental import pallas as pl
from jax.experimental.pallas import tpu as pltpu
from jax.sharding import Mesh
from jax.sharding import PartitionSpec as P

K = 9
RAD = 2
WIDTH = 2 * RAD + 1
TAPS = WIDTH * WIDTH
ROWS = 4
PLACES = ROWS + 2 * RAD
NJ = 512
C = 256
J = 32
STEPS = NJ // J
EDGE = 16
EXT_WINDOW = 48
EXT = NJ + 16
DEPTH = WIDTH * EXT_WINDOW
WIDE = NJ + 2 * EDGE + 16
LANES = 128
BLOCKS = 2 * K
PADDED_BLOCKS = 20
MIB = 1024 * 1024
BF = jnp.bfloat16
F32 = jnp.float32

IN_VMEM = pl.BlockSpec(memory_space=pltpu.VMEM)
IN_SMEM = pl.BlockSpec(memory_space=pltpu.SMEM)
IN_HBM = pl.BlockSpec(memory_space=pltpu.HBM)
ANYWHERE = pl.BlockSpec(memory_space=pl.ANY)


def in_hbm(array):
    return pltpu.with_memory_space_constraint(array, pltpu.HBM)


def params(mib):
    return pltpu.CompilerParams(vmem_limit_bytes=mib * MIB)


def cost(flops, moved):
    return pl.CostEstimate(flops=int(flops), bytes_accessed=int(moved), transcendentals=0)


def banded(line):
    return pltpu.roll(jnp.broadcast_to(line, (J, 256)), 0, axis=1, stride=1, stride_axis=0).astype(BF)


def one_hot(lane_of_tap):
    tap = lax.broadcasted_iota(jnp.int32, (LANES, 256), 0)
    lane = lax.broadcasted_iota(jnp.int32, (LANES, 256), 1)
    return jnp.where((lane == lane_of_tap(tap)) & (tap < TAPS), 1.0, 0.0).astype(BF)


def send_kernel(lo_ref, hi_ref, basis_ref, feat_ref, cot_ref, chip_ref, link_ref, right_ref, left_ref, kept_ref, lo, hi, basis, sems):
    core = lax.axis_index("core")
    to_chip, to_link = 2 - 2 * core, 2 * core
    copies = [
        (lo_ref, lo),
        (hi_ref, hi),
        (basis_ref, basis),
        (feat_ref.at[pl.ds(to_link, 2)], link_ref),
        (feat_ref.at[pl.ds(to_chip, 2)], chip_ref),
        (cot_ref.at[:, pl.ds(NJ - EDGE, EDGE)], right_ref),
        (cot_ref.at[:, pl.ds(0, EDGE)], left_ref),
    ]
    copies = [pltpu.make_async_copy(a, b, sems.at[n]) for n, (a, b) in enumerate(copies)]
    for copy in copies:
        copy.start()
    offset = lax.broadcasted_iota(jnp.int32, (16, LANES), 1) // WIDTH - RAD
    for copy in copies[:3]:
        copy.wait()
    for i in range(ROWS):
        cells = jnp.pad(basis[:, i, :], ((0, 16 - K), (0, LANES - TAPS)))
        cells = jnp.where((offset >= lo[i]) & (offset <= hi[i]), cells, jnp.zeros_like(cells))
        kept_ref[i] = cells.astype(BF)
    for copy in copies[3:]:
        copy.wait()


def send_part(span_lo, span_hi, basis, features, cotangent):
    basis = jnp.transpose(basis, (1, 0, 2))
    return pl.pallas_call(
        send_kernel,
        out_shape=(
            pltpu.VMEM((2, NJ, C), BF),
            pltpu.VMEM((2, NJ, C), BF),
            pltpu.VMEM((ROWS, EDGE, C), BF),
            pltpu.VMEM((ROWS, EDGE, C), BF),
            pltpu.VMEM((ROWS, 16, LANES), BF),
        ),
        in_specs=[IN_HBM] * 5,
        out_specs=[IN_VMEM] * 5,
        scratch_shapes=[
            pltpu.SMEM((ROWS,), jnp.int32),
            pltpu.SMEM((ROWS,), jnp.int32),
            pltpu.VMEM(basis.shape, F32),
            pltpu.SemaphoreType.DMA((7,)),
        ],
        compiler_params=params(4),
        cost_estimate=cost(0, 2e6),
        name="send_part",
    )(in_hbm(span_lo), in_hbm(span_hi), in_hbm(basis), in_hbm(features), in_hbm(cotangent))


def own_kernel(kept_ref, cot_ref, feat_ref, weight_hbm, turned_ref, extended_ref, bands_ref, weight_ref, sem):
    weight_copy = pltpu.make_async_copy(weight_hbm, weight_ref, sem)
    weight_copy.start()
    turned_ref[...] = cot_ref[...].reshape(ROWS * NJ, C).T
    gap = jnp.zeros((8, C), BF)
    for i in range(ROWS):
        extended_ref[i] = jnp.concatenate([gap, feat_ref[i], gap], axis=0)
    place = one_hot(lambda tap: tap // WIDTH * EXT_WINDOW + 8 - RAD + tap % WIDTH)
    for i in range(ROWS):
        line = jnp.dot(kept_ref[i], place, preferred_element_type=F32)
        for k in range(K):
            bands_ref[i, k * J : (k + 1) * J, :] = banded(line[k : k + 1, :])[:, :DEPTH]
    weight_copy.wait()


def own_part(kept, cotangent, features, weight):
    return pl.pallas_call(
        own_kernel,
        out_shape=(
            pltpu.VMEM((C, ROWS * NJ), BF),
            pltpu.VMEM((ROWS, EXT, C), BF),
            pltpu.VMEM((ROWS, K * J, DEPTH), BF),
            pltpu.VMEM((K * C, C), BF),
        ),
        in_specs=[IN_VMEM] * 3 + [IN_HBM],
        out_specs=[IN_VMEM] * 4,
        scratch_shapes=[pltpu.SemaphoreType.DMA(())],
        compiler_params=params(4),
        cost_estimate=cost(1e9, 4e6),
        name="own_part",
    )(kept, cotangent, features, in_hbm(weight))


def halo_kernel(chip_ref, link_ref, left_ref, right_ref, turned_ref, extended_ref, bands_ref, kept_ref, cot_ref, own_ref, other_ref, filtered, chip_cot_ref, link_cot_ref, halo, total, kept, sems):
    core = lax.axis_index("core")
    copies = []
    for n, (ref, first) in enumerate(((chip_cot_ref, 2 - 2 * core), (link_cot_ref, 2 * core))):
        kept[n] = jnp.zeros((2, 16, C), BF)
        for i in range(2):
            kept[n, i, :, 0:LANES] = kept_ref[first + i]
        pair = pl.ds(first, 2)
        for source, start, size in (
            (left_ref.at[pair], 0, EDGE),
            (cot_ref.at[pair], EDGE, NJ),
            (right_ref.at[pair], EDGE + NJ, EDGE),
            (kept.at[n], 2 * EDGE + NJ, 16),
        ):
            copies.append(
                pltpu.make_async_copy(source, ref.at[:, pl.ds(start, size)], sems.at[len(copies)])
            )
    for copy in copies:
        copy.start()
    gap = jnp.zeros((8, C), BF)

    def fill(low, high):
        for n in range(2):
            extend(halo, n, low[n], gap, gap)
            extend(halo, 2 + n, high[n], gap, gap)

    pl.when(core == 0)(lambda: fill(link_ref, chip_ref))
    pl.when(core == 1)(lambda: fill(chip_ref, link_ref))
    rows = [halo.at[0], halo.at[1]] + [extended_ref.at[i] for i in range(ROWS)] + [halo.at[2], halo.at[3]]
    middle = jnp.zeros((EXT_WINDOW - 16, C), BF)
    for row in range(ROWS):
        for tile in range(STEPS + 1):
            if tile < STEPS:
                start = tile * J
                first = row * NJ + start
                cells = [rows[row + r][start : start + EXT_WINDOW, :] for r in range(WIDTH)]
            else:
                first = ROWS * NJ + row * J
                cells = []
                for r in range(WIDTH):
                    cells += [rows[row + r][NJ : NJ + 8, :], middle, rows[row + r][8:16, :]]
            found = jnp.dot(
                bands_ref[row], jnp.concatenate(cells, axis=0), preferred_element_type=F32
            ).astype(BF)
            for k in range(K):
                filtered[first : first + J, k * C : (k + 1) * C] = found[k * J : (k + 1) * J]
    edges = [piece for i in range(ROWS) for piece in (right_ref[i], left_ref[i])]
    edges = jnp.concatenate(edges, axis=0).T
    for k in range(K):
        columns = slice(k * C, (k + 1) * C)
        total[:, columns] = jnp.dot(
            turned_ref[...], filtered[0 : ROWS * NJ, columns], preferred_element_type=F32
        ) + jnp.dot(edges, filtered[ROWS * NJ :, columns], preferred_element_type=F32)
    mine = pl.multiple_of(core * LANES, LANES)
    theirs = pl.multiple_of((1 - core) * LANES, LANES)
    for block in range(BLOCKS):
        columns = slice(block * LANES, (block + 1) * LANES)
        own_ref[block] = total[pl.ds(mine, LANES), columns]
        other_ref[block] = total[pl.ds(theirs, LANES), columns].astype(BF)
    for block in range(BLOCKS, PADDED_BLOCKS):
        own_ref[block] = jnp.zeros((LANES, LANES), F32)
        other_ref[block] = jnp.zeros((LANES, LANES), BF)
    for copy in copies:
        copy.wait()


def halo_part(chip, link, left, right, turned, extended, bands, kept, cotangent):
    shape = (PADDED_BLOCKS, LANES, LANES)
    return pl.pallas_call(
        halo_kernel,
        out_shape=(
            pltpu.VMEM(shape, F32),
            pltpu.VMEM(shape, BF),
            pltpu.VMEM((ROWS * (NJ + J), K * C), BF),
            pltpu.VMEM((2, WIDE, C), BF),
            pltpu.VMEM((2, WIDE, C), BF),
        ),
        in_specs=[IN_VMEM] * 8 + [IN_HBM],
        out_specs=[IN_VMEM] * 5,
        scratch_shapes=[
            pltpu.VMEM((ROWS, EXT, C), BF),
            pltpu.VMEM((C, K * C), F32),
            pltpu.VMEM((2, 2, 16, C), BF),
            pltpu.SemaphoreType.DMA((8,)),
        ],
        compiler_params=params(14),
        cost_estimate=cost(8e9, 4e6),
        name="halo_part",
    )(chip, link, left, right, turned, extended, bands, kept, in_hbm(cotangent))


def half_kernel(own_ref, other_ref, _, out_ref):
    out_ref[...] = (own_ref[...] + other_ref[...].astype(F32)).astype(BF)


def half_part(own, other, after):
    return pl.pallas_call(
        half_kernel,
        out_shape=pltpu.VMEM(own.shape, BF),
        in_specs=[IN_VMEM] * 2 + [ANYWHERE],
        out_specs=IN_VMEM,
        compiler_params=params(4),
        cost_estimate=cost(1e6, 3e6),
        name="half_part",
    )(own, other, after)


def mixed_kernel(filtered_ref, weight_ref, out_ref, ends_ref, to_right_ref, to_left_ref, mixed, sems):
    copies = [pltpu.make_async_copy(mixed.at[row], out_ref.at[row], sems.at[row]) for row in range(ROWS)]
    beyond = jnp.dot(filtered_ref[ROWS * NJ :, :], weight_ref[...], preferred_element_type=F32)
    for row in range(ROWS):
        to_right_ref[row] = beyond[row * J : row * J + EDGE]
        to_left_ref[row] = beyond[row * J + EDGE : (row + 1) * J]
        found = jnp.dot(
            filtered_ref[row * NJ : (row + 1) * NJ, :], weight_ref[...], preferred_element_type=F32
        )
        ends_ref[row, 0:EDGE, :] = found[0:EDGE]
        ends_ref[row, EDGE:, :] = found[NJ - EDGE :]
        mixed[row] = found.astype(BF)
        copies[row].start()
    for copy in copies:
        copy.wait()


def mixed_part(filtered, weight):
    return pl.pallas_call(
        mixed_kernel,
        out_shape=(
            jax.ShapeDtypeStruct((ROWS, NJ, C), BF),
            pltpu.VMEM((ROWS, 2 * EDGE, C), F32),
            pltpu.VMEM((ROWS, EDGE, C), F32),
            pltpu.VMEM((ROWS, EDGE, C), F32),
        ),
        in_specs=[IN_VMEM] * 2,
        out_specs=[IN_HBM] + [IN_VMEM] * 3,
        scratch_shapes=[pltpu.VMEM((ROWS, NJ, C), BF), pltpu.SemaphoreType.DMA((ROWS,))],
        compiler_params=params(6),
        cost_estimate=cost(1e9, 2e6),
        name="mixed_part",
    )(filtered, weight)


def ends_kernel(ends_ref, left_ref, right_ref, _, __, out_ref, done_ref, ends, sems):
    ends[0] = (ends_ref[:, 0:EDGE, :] + left_ref[...]).astype(BF)
    ends[1] = (ends_ref[:, EDGE:, :] + right_ref[...]).astype(BF)
    copies = [
        pltpu.make_async_copy(ends.at[n], out_ref.at[:, pl.ds(first, EDGE)], sems.at[n])
        for n, first in enumerate((0, NJ - EDGE))
    ]
    for copy in copies:
        copy.start()
    done_ref[...] = jnp.zeros_like(done_ref)
    for copy in copies:
        copy.wait()


def ends_part(ends, left, right, mixed, after):
    return pl.pallas_call(
        ends_kernel,
        out_shape=(jax.ShapeDtypeStruct(mixed.shape, BF), pltpu.VMEM((8, LANES), F32)),
        in_specs=[IN_VMEM] * 3 + [IN_HBM, ANYWHERE],
        out_specs=[IN_HBM, IN_VMEM],
        input_output_aliases={3: 0},
        scratch_shapes=[pltpu.VMEM((2, ROWS, EDGE, C), BF), pltpu.SemaphoreType.DMA((2,))],
        compiler_params=params(4),
        cost_estimate=cost(1e6, 1e6),
        name="ends_part",
    )(ends, left, right, mixed, after)


def sum_kernel(scale, pieces_ref, out_ref):
    piece = (jnp.sum(pieces_ref[...].astype(F32), axis=0) * scale).astype(BF)
    out_ref[...] = jnp.broadcast_to(piece, out_ref.shape)


def sum_part(pieces, scale):
    return pl.pallas_call(
        functools.partial(sum_kernel, scale),
        out_shape=pltpu.VMEM(pieces.shape, BF),
        in_specs=[IN_VMEM],
        out_specs=IN_VMEM,
        compiler_params=params(4),
        cost_estimate=cost(1e6, 2e6),
        name="sum_part",
    )(pieces)


def order_kernel(*_):
    pass


def ordered(value, after):
    return pl.pallas_call(
        order_kernel,
        out_shape=jax.ShapeDtypeStruct(value.shape, value.dtype),
        in_specs=[ANYWHERE, ANYWHERE],
        out_specs=ANYWHERE,
        input_output_aliases={0: 0},
        compiler_params=params(1),
        name="ordered",
    )(value, after)


def result_kernel(own_ref, other_ref, out_ref):
    core = lax.axis_index("core")
    for n in range(out_ref.shape[0]):
        for part in range(2):
            rows = slice(part * LANES, (part + 1) * LANES)
            mine = own_ref[2 * n + part].astype(F32).T
            theirs = other_ref[2 * n + part].astype(F32).T
            out_ref[n, rows, 0:LANES] = jnp.where(core == 0, mine, theirs)
            out_ref[n, rows, LANES:] = jnp.where(core == 0, theirs, mine)


def result_part(own, other):
    step = 3
    return pl.pallas_call(
        result_kernel,
        grid=(K // step,),
        out_shape=jax.ShapeDtypeStruct((K, C, C), F32),
        in_specs=[pl.BlockSpec((2 * step, LANES, LANES), lambda n: (n, 0, 0))] * 2,
        out_specs=pl.BlockSpec((step, C, C), lambda n: (n, 0, 0)),
        compiler_params=params(6),
        cost_estimate=cost(1e6, 4e6),
        name="result_part",
    )(own, other)


def extend(extended, n, row, left, right):
    extended[n] = jnp.concatenate([left, row, right], axis=0)


def grad_kernel(kept_ref, chip_ref, link_ref, left_ref, right_ref, weight_hbm, cot_hbm, _, out_ref, done_ref, weight, weight_turned, cot, extended, bands, cells, filtered, mixed, sems):
    core = lax.axis_index("core")
    cot_copy = pltpu.make_async_copy(cot_hbm, cot, sems.at[ROWS])
    cot_copy.start()
    weight_copy = pltpu.make_async_copy(weight_hbm, weight, sems.at[ROWS + 1])
    weight_copy.start()

    def fill(low, high):
        for n in range(2):
            extended[n] = low[n, 8 : 8 + EXT, :]
            extended[6 + n] = high[n, 8 : 8 + EXT, :]
            cells[n] = low[n, 2 * EDGE + NJ :, 0:LANES]
            cells[6 + n] = high[n, 2 * EDGE + NJ :, 0:LANES]

    pl.when(core == 0)(lambda: fill(link_ref, chip_ref))
    pl.when(core == 1)(lambda: fill(chip_ref, link_ref))
    for n in range(ROWS):
        cells[2 + n] = kept_ref[n]

    away = (TAPS - 1 - lax.broadcasted_iota(jnp.int32, (16, LANES), 1)) // WIDTH
    place = one_hot(lambda tap: (TAPS - 1 - tap) // WIDTH * EXT_WINDOW + 8 - RAD + (TAPS - 1 - tap) % WIDTH)
    lines = []
    for row in range(ROWS):
        taken = jnp.zeros((16, LANES), F32)
        for r in range(WIDTH):
            taken = jnp.where(away == r, cells[row + r].astype(F32), taken)
        lines.append(jnp.dot(taken.astype(BF), place, preferred_element_type=F32))
    cot_copy.wait()
    for n in range(ROWS):
        extend(extended, 2 + n, cot[n], left_ref[n, 8:, :], right_ref[n, :8, :])
    copies = [pltpu.make_async_copy(mixed.at[row], out_ref.at[row], sems.at[row]) for row in range(ROWS)]
    for row in range(ROWS):
        slot = row % 2
        for k in range(K):
            bands[slot, k * J : (k + 1) * J, :] = banded(lines[row][k : k + 1, :])[:, :DEPTH]
        for tile in range(STEPS):
            start = tile * J
            window = jnp.concatenate(
                [extended[row + r, start : start + EXT_WINDOW, :] for r in range(WIDTH)], axis=0
            )
            found = jnp.dot(bands[slot], window, preferred_element_type=F32).astype(BF)
            for k in range(K):
                filtered[slot, start : start + J, k * C : (k + 1) * C] = found[k * J : (k + 1) * J]
        if row == 0:
            weight_copy.wait()
            for k in range(K):
                columns = slice(k * C, (k + 1) * C)
                weight_turned[columns, :] = weight[columns, :].T
        mixed[row] = jnp.dot(filtered[slot], weight_turned[...], preferred_element_type=F32).astype(BF)
        copies[row].start()
    for copy in copies:
        copy.wait()
    done_ref[...] = jnp.zeros_like(done_ref)


def grad_part(kept, chip, link, left, right, weight, cotangent, after):
    return pl.pallas_call(
        grad_kernel,
        out_shape=(jax.ShapeDtypeStruct((ROWS, NJ, C), BF), pltpu.VMEM((8, LANES), F32)),
        in_specs=[IN_VMEM] * 5 + [IN_HBM, IN_HBM, ANYWHERE],
        out_specs=[IN_HBM, IN_VMEM],
        scratch_shapes=[
            pltpu.VMEM((K * C, C), BF),
            pltpu.VMEM((K * C, C), BF),
            pltpu.VMEM((ROWS, NJ, C), BF),
            pltpu.VMEM((PLACES, EXT, C), BF),
            pltpu.VMEM((2, K * J, DEPTH), BF),
            pltpu.VMEM((PLACES, 16, LANES), BF),
            pltpu.VMEM((2, NJ, K * C), BF),
            pltpu.VMEM((ROWS, NJ, C), BF),
            pltpu.SemaphoreType.DMA((ROWS + 2,)),
        ],
        compiler_params=params(20),
        cost_estimate=cost(8e9, 5e6),
        name="grad_input_part",
    )(kept, chip, link, left, right, in_hbm(weight), in_hbm(cotangent), after)


def shifted(block, axis, count, step, periodic):
    route = [(i, (i + step) % count) for i in range(count) if periodic or 0 <= i + step < count]
    return lax.ppermute(block, axis, route)


def per_device(features, basis, span_lo, span_hi, weight, cotangent):
    lat, chips = ("yz", "core"), ("yz", "lon")
    lats, lons = lax.axis_size("yz") * lax.axis_size("core"), lax.axis_size("lon")
    parts = lax.axis_size("yz") * lons
    swap = [(0, 1), (1, 0)]

    pairs = [(i, i + 1) for i in range(1, lats - 1, 2)]
    pairs = pairs + [(b, a) for a, b in pairs]
    chip, link, to_right, to_left, kept = send_part(span_lo, span_hi, basis, features, cotangent)
    link = lax.ppermute(link, lat, pairs)
    chip = lax.ppermute(chip, "core", swap)
    near_left = shifted(to_right, "lon", lons, 1, True)
    near_right = shifted(to_left, "lon", lons, -1, True)
    weight = weight.reshape(K * C, C)
    turned, extended, bands, weight_near = own_part(kept, cotangent, features, weight)
    own, other, filtered, chip_cot, link_cot = halo_part(
        chip, link, near_left, near_right, turned, extended, bands, kept, cotangent
    )

    other = lax.ppermute(other, "core", swap)
    mixed, ends, to_right, to_left = mixed_part(filtered, weight_near)
    half = half_part(own, other, ends)
    pieces = lax.all_to_all(half.reshape(parts, -1, LANES), chips, 0, 0)
    link_cot = lax.ppermute(ordered(link_cot, half), lat, pairs)
    chip_cot = lax.ppermute(ordered(chip_cot, half), "core", swap)
    left = shifted(ordered(to_right, half), "lon", lons, 1, True)
    right = shifted(ordered(to_left, half), "lon", lons, -1, True)
    scale = 1.0 / math.sqrt(ROWS * lats * NJ * lons)
    copies = sum_part(pieces, scale)
    gathered = lax.all_to_all(copies, chips, 0, 0).reshape(PADDED_BLOCKS, LANES, LANES)
    mixed, mixed_done = ends_part(ends, left, right, mixed, copies)
    grad_input, grad_done = grad_part(
        kept, chip_cot, link_cot, near_left, near_right, weight, cotangent, mixed_done
    )
    gathered = ordered(gathered, grad_done)
    grad_weight = result_part(gathered, lax.ppermute(gathered, "core", swap))
    return mixed, grad_input, grad_weight


def solution(mesh):
    lats, lons = mesh.devices.shape
    split = Mesh(mesh.devices.reshape(lats // 2, 2, lons), ("yz", "core", "lon"))
    lat = ("yz", "core")
    return jax.shard_map(
        per_device,
        mesh=split,
        in_specs=(P(lat, "lon", None), P(lat, None, None), P(lat), P(lat), P(), P(lat, "lon", None)),
        out_specs=(P(lat, "lon", None), P(lat, "lon", None), P()),
        check_vma=False,
    )
```

```python
import functools
import math

import jax
import jax.numpy as jnp
from jax import lax
from jax.experimental import pallas as pl
from jax.experimental.pallas import tpu as pltpu
from jax.sharding import Mesh
from jax.sharding import PartitionSpec as P

K = 9
RAD = 2
WIDTH = 2 * RAD + 1
TAPS = WIDTH * WIDTH
ROWS = 4
PLACES = ROWS + 2 * RAD
NJ = 512
C = 256
J = 32
STEPS = NJ // J
EDGE = 16
EXT_WINDOW = 48
EXT = NJ + 16
DEPTH = WIDTH * EXT_WINDOW
WIDE = NJ + 2 * EDGE + 16
LANES = 128
BLOCKS = 2 * K
PADDED_BLOCKS = 20
MIB = 1024 * 1024
BF = jnp.bfloat16
F32 = jnp.float32

IN_VMEM = pl.BlockSpec(memory_space=pltpu.VMEM)
IN_SMEM = pl.BlockSpec(memory_space=pltpu.SMEM)
IN_HBM = pl.BlockSpec(memory_space=pltpu.HBM)
ANYWHERE = pl.BlockSpec(memory_space=pl.ANY)


def in_hbm(array):
    return pltpu.with_memory_space_constraint(array, pltpu.HBM)


def params(mib):
    return pltpu.CompilerParams(vmem_limit_bytes=mib * MIB)


def cost(flops, moved):
    return pl.CostEstimate(flops=int(flops), bytes_accessed=int(moved), transcendentals=0)


def banded(line):
    return pltpu.roll(jnp.broadcast_to(line, (J, 256)), 0, axis=1, stride=1, stride_axis=0).astype(BF)


def one_hot(lane_of_tap):
    tap = lax.broadcasted_iota(jnp.int32, (LANES, 256), 0)
    lane = lax.broadcasted_iota(jnp.int32, (LANES, 256), 1)
    return jnp.where((lane == lane_of_tap(tap)) & (tap < TAPS), 1.0, 0.0).astype(BF)


def send_kernel(feat_ref, chip_ref, link_ref, sems):
    core = lax.axis_index("core")
    copies = [
        pltpu.make_async_copy(feat_ref.at[pl.ds(first, 2)], ref, sems.at[n])
        for n, (ref, first) in enumerate(((link_ref, 2 * core), (chip_ref, 2 - 2 * core)))
    ]
    for copy in copies:
        copy.start()
    for copy in copies:
        copy.wait()


def send_part(features):
    return pl.pallas_call(
        send_kernel,
        out_shape=(pltpu.VMEM((2, NJ, C), BF), pltpu.VMEM((2, NJ, C), BF)),
        in_specs=[IN_HBM],
        out_specs=[IN_VMEM] * 2,
        scratch_shapes=[pltpu.SemaphoreType.DMA((2,))],
        compiler_params=params(2),
        cost_estimate=cost(0, 1e6),
        name="send_part",
    )(in_hbm(features))


def own_kernel(lo_ref, hi_ref, basis_ref, cot_ref, feat_ref, _, to_right_ref, to_left_ref, kept_ref, turned_ref, extended_ref, bands_ref, lo, hi, basis, cot, feat, sems):
    copies = (
        (lo_ref, lo),
        (hi_ref, hi),
        (basis_ref, basis),
        (cot_ref, cot),
        (feat_ref, feat),
    )
    copies = [pltpu.make_async_copy(a, b, sems.at[n]) for n, (a, b) in enumerate(copies)]
    for copy in copies:
        copy.start()
    place = one_hot(lambda tap: tap // WIDTH * EXT_WINDOW + 8 - RAD + tap % WIDTH)
    offset = lax.broadcasted_iota(jnp.int32, (16, LANES), 1) // WIDTH - RAD
    for copy in copies[:3]:
        copy.wait()
    for i in range(ROWS):
        cells = jnp.pad(basis[:, i, :], ((0, 16 - K), (0, LANES - TAPS)))
        cells = jnp.where((offset >= lo[i]) & (offset <= hi[i]), cells, jnp.zeros_like(cells)).astype(BF)
        kept_ref[i] = cells
        line = jnp.dot(cells, place, preferred_element_type=F32)
        for k in range(K):
            bands_ref[i, k * J : (k + 1) * J, :] = banded(line[k : k + 1, :])[:, :DEPTH]
    copies[3].wait()
    to_right_ref[...] = cot[:, NJ - EDGE :, :]
    to_left_ref[...] = cot[:, :EDGE, :]
    for pair in range(2):
        turned_ref[pair] = cot[2 * pair : 2 * pair + 2].reshape(2 * NJ, C).T
    copies[4].wait()
    gap = jnp.zeros((8, C), BF)
    for i in range(ROWS):
        extended_ref[i] = jnp.concatenate([gap, feat[i], gap], axis=0)


def own_part(span_lo, span_hi, basis, cotangent, features, after):
    basis = jnp.transpose(basis, (1, 0, 2))
    return pl.pallas_call(
        own_kernel,
        out_shape=(
            pltpu.VMEM((ROWS, EDGE, C), BF),
            pltpu.VMEM((ROWS, EDGE, C), BF),
            pltpu.VMEM((ROWS, 16, LANES), BF),
            pltpu.VMEM((2, C, 2 * NJ), BF),
            pltpu.VMEM((ROWS, EXT, C), BF),
            pltpu.VMEM((ROWS, K * J, DEPTH), BF),
        ),
        in_specs=[IN_HBM] * 5 + [ANYWHERE],
        out_specs=[IN_VMEM] * 6,
        scratch_shapes=[
            pltpu.SMEM((ROWS,), jnp.int32),
            pltpu.SMEM((ROWS,), jnp.int32),
            pltpu.VMEM(basis.shape, F32),
            pltpu.VMEM((ROWS, NJ, C), BF),
            pltpu.VMEM((ROWS, NJ, C), BF),
            pltpu.SemaphoreType.DMA((5,)),
        ],
        compiler_params=params(6),
        cost_estimate=cost(4e9, 4e6),
        name="own_part",
    )(*map(in_hbm, (span_lo, span_hi, basis, cotangent, features)), after)


def row_pair(side):
    core = lax.axis_index("core")
    return core if side == 0 else 1 - core


def filter_kernel(side, halo_ref, extended_ref, bands_ref, *refs):
    copies = []
    if side == 0:
        turned_ref, weight_hbm, total_ref, filtered, weight_ref, rows, sem = refs
        copies.append(pltpu.make_async_copy(weight_hbm, weight_ref, sem))
    else:
        turned_ref, before_ref, kept_ref, cot_ref, total_ref, filtered, chip_cot_ref, link_cot_ref, rows, kept, sems = refs
        core = lax.axis_index("core")
        for n, (ref, first) in enumerate(((chip_cot_ref, 2 - 2 * core), (link_cot_ref, 2 * core))):
            kept[n] = jnp.zeros((2, 16, C), BF)
            for i in range(2):
                kept[n, i, :, 0:LANES] = kept_ref[first + i]
            for source, start, size in ((cot_ref.at[pl.ds(first, 2)], EDGE, NJ), (kept.at[n], 2 * EDGE + NJ, 16)):
                target = ref.at[:, pl.ds(start, size)]
                copies.append(pltpu.make_async_copy(source, target, sems.at[len(copies)]))
    for copy in copies:
        copy.start()
    pair = row_pair(side)
    gap = jnp.zeros((8, C), BF)
    for n in range(2):
        rows[4 - 4 * pair + n] = jnp.concatenate([gap, halo_ref[n], gap], axis=0)
    for n in range(ROWS):
        rows[2 * pair + n] = extended_ref[n]
    middle = jnp.zeros((EXT_WINDOW - 16, C), BF)
    for row in range(2):
        bands = bands_ref[2 - 2 * pair + row]
        for tile in range(STEPS + 1):
            if tile < STEPS:
                start = tile * J
                first = row * NJ + start
                cells = [rows[row + r, start : start + EXT_WINDOW, :] for r in range(WIDTH)]
            else:
                first = 2 * NJ + row * J
                cells = []
                for r in range(WIDTH):
                    cells += [rows[row + r, NJ : NJ + 8, :], middle, rows[row + r, 8:16, :]]
            found = jnp.dot(bands, jnp.concatenate(cells, axis=0), preferred_element_type=F32).astype(BF)
            for k in range(K):
                filtered[first : first + J, k * C : (k + 1) * C] = found[k * J : (k + 1) * J]
    for k in range(K):
        columns = slice(k * C, (k + 1) * C)
        part = jnp.dot(turned_ref[1 - pair], filtered[0 : 2 * NJ, columns], preferred_element_type=F32)
        total_ref[:, columns] = part if side == 0 else before_ref[:, columns] + part
    for copy in copies:
        copy.wait()


def filter_part(side, *operands):
    outs = [pltpu.VMEM((C, K * C), F32), pltpu.VMEM((2 * (NJ + J), K * C), BF)]
    scratch = [pltpu.VMEM((6, EXT, C), BF)]
    if side == 0:
        outs += [pltpu.VMEM((K * C, C), BF)]
        scratch += [pltpu.SemaphoreType.DMA(())]
    else:
        outs += [pltpu.VMEM((2, WIDE, C), BF)] * 2
        scratch += [pltpu.VMEM((2, 2, 16, C), BF), pltpu.SemaphoreType.DMA((4,))]
    return pl.pallas_call(
        functools.partial(filter_kernel, side),
        out_shape=tuple(outs),
        in_specs=[IN_VMEM] * (len(operands) - 1) + [IN_HBM],
        out_specs=[IN_VMEM] * len(outs),
        scratch_shapes=scratch,
        compiler_params=params(8),
        cost_estimate=cost(1e8, 1e5),
        name="filter_part",
    )(*operands[:-1], in_hbm(operands[-1]))


def edge_kernel(left_ref, right_ref, total_ref, near_ref, far_ref, _, __, own_ref, other_ref, chip_cot_ref, link_cot_ref, sems):
    core = lax.axis_index("core")
    copies = []
    for ref, first in ((chip_cot_ref, 2 - 2 * core), (link_cot_ref, 2 * core)):
        for source, start in ((left_ref, 0), (right_ref, EDGE + NJ)):
            target = ref.at[:, pl.ds(start, EDGE)]
            copies.append(pltpu.make_async_copy(source.at[pl.ds(first, 2)], target, sems.at[len(copies)]))
    for copy in copies:
        copy.start()
    edges = []
    for side in range(2):
        for row in range(2):
            i = 2 - 2 * row_pair(side) + row
            edges += [right_ref[i], left_ref[i]]
    edges = jnp.concatenate(edges, axis=0).T
    for k in range(K):
        columns = slice(k * C, (k + 1) * C)
        beyond = jnp.concatenate([near_ref[2 * NJ :, columns], far_ref[2 * NJ :, columns]], axis=0)
        total = total_ref[:, columns] + jnp.dot(edges, beyond, preferred_element_type=F32)
        first, second = total[:LANES], total[LANES:]
        mine = jnp.where(core == 0, first, second)
        theirs = jnp.where(core == 0, second, first).astype(BF)
        for part in range(2):
            lanes = slice(part * LANES, (part + 1) * LANES)
            own_ref[2 * k + part] = mine[:, lanes]
            other_ref[2 * k + part] = theirs[:, lanes]
    for block in range(BLOCKS, PADDED_BLOCKS):
        own_ref[block] = jnp.zeros((LANES, LANES), F32)
        other_ref[block] = jnp.zeros((LANES, LANES), BF)
    for copy in copies:
        copy.wait()


def edge_part(left, right, total, near, far, chip_cot, link_cot):
    shape = (PADDED_BLOCKS, LANES, LANES)
    return pl.pallas_call(
        edge_kernel,
        out_shape=(
            pltpu.VMEM(shape, F32),
            pltpu.VMEM(shape, BF),
            pltpu.VMEM((2, WIDE, C), BF),
            pltpu.VMEM((2, WIDE, C), BF),
        ),
        in_specs=[IN_VMEM] * 5 + [ANYWHERE] * 2,
        out_specs=[IN_VMEM] * 2 + [ANYWHERE] * 2,
        input_output_aliases={5: 2, 6: 3},
        scratch_shapes=[pltpu.SemaphoreType.DMA((4,))],
        compiler_params=params(4),
        cost_estimate=cost(1e9, 4e6),
        name="edge_part",
    )(left, right, total, near, far, chip_cot, link_cot)


def half_kernel(own_ref, other_ref, _, out_ref, half, sems):
    copies = []
    for n in range(4):
        part = pl.ds(n * PADDED_BLOCKS // 4, PADDED_BLOCKS // 4)
        half[part] = (own_ref[part] + other_ref[part].astype(F32)).astype(BF)
        copies.append(pltpu.make_async_copy(half.at[part], out_ref.at[part], sems.at[n]))
        copies[n].start()
    for copy in copies:
        copy.wait()


def half_part(own, other, after):
    return pl.pallas_call(
        half_kernel,
        out_shape=jax.ShapeDtypeStruct(own.shape, BF),
        in_specs=[IN_VMEM] * 2 + [ANYWHERE],
        out_specs=IN_HBM,
        scratch_shapes=[pltpu.VMEM(own.shape, BF), pltpu.SemaphoreType.DMA((4,))],
        compiler_params=params(4),
        cost_estimate=cost(1e6, 3e6),
        name="half_part",
    )(own, other, after)


def mixed_kernel(near_ref, far_ref, weight_ref, mixed_ref, ends_ref, to_right_ref, to_left_ref):
    for side, filtered_ref in enumerate((near_ref, far_ref)):
        first = 2 - 2 * row_pair(side)
        beyond = jnp.dot(filtered_ref[2 * NJ :, :], weight_ref[...], preferred_element_type=F32)
        for row in range(2):
            to_right_ref[first + row] = beyond[row * J : row * J + EDGE]
            to_left_ref[first + row] = beyond[row * J + EDGE : (row + 1) * J]
            found = jnp.dot(
                filtered_ref[row * NJ : (row + 1) * NJ, :], weight_ref[...], preferred_element_type=F32
            )
            ends_ref[first + row, 0:EDGE, :] = found[0:EDGE]
            ends_ref[first + row, EDGE:, :] = found[NJ - EDGE :]
            mixed_ref[first + row] = found.astype(BF)


def mixed_part(near, far, weight):
    return pl.pallas_call(
        mixed_kernel,
        out_shape=(
            pltpu.VMEM((ROWS, NJ, C), BF),
            pltpu.VMEM((ROWS, 2 * EDGE, C), F32),
            pltpu.VMEM((ROWS, EDGE, C), F32),
            pltpu.VMEM((ROWS, EDGE, C), F32),
        ),
        in_specs=[IN_VMEM] * 3,
        out_specs=[IN_VMEM] * 4,
        compiler_params=params(4),
        cost_estimate=cost(1e9, 2e6),
        name="mixed_part",
    )(near, far, weight)


def ends_kernel(ends_ref, left_ref, right_ref, mixed_ref, _, out_ref, done_ref, ends, sems):
    middle = pl.ds(EDGE, NJ - 2 * EDGE)
    copies = [pltpu.make_async_copy(mixed_ref.at[:, middle], out_ref.at[:, middle], sems.at[2])]
    copies[0].start()
    ends[0] = (ends_ref[:, 0:EDGE, :] + left_ref[...]).astype(BF)
    ends[1] = (ends_ref[:, EDGE:, :] + right_ref[...]).astype(BF)
    for n, first in enumerate((0, NJ - EDGE)):
        target = out_ref.at[:, pl.ds(first, EDGE)]
        copies.append(pltpu.make_async_copy(ends.at[n], target, sems.at[n]))
        copies[-1].start()
    done_ref[...] = jnp.zeros_like(done_ref)
    for copy in copies:
        copy.wait()


def ends_part(ends, left, right, mixed, after):
    return pl.pallas_call(
        ends_kernel,
        out_shape=(jax.ShapeDtypeStruct(mixed.shape, BF), pltpu.VMEM((8, LANES), F32)),
        in_specs=[IN_VMEM] * 4 + [ANYWHERE],
        out_specs=[IN_HBM, IN_VMEM],
        scratch_shapes=[pltpu.VMEM((2, ROWS, EDGE, C), BF), pltpu.SemaphoreType.DMA((3,))],
        compiler_params=params(4),
        cost_estimate=cost(1e6, 1e6),
        name="ends_part",
    )(ends, left, right, mixed, after)


def sum_kernel(scale, pieces_ref, out_ref):
    piece = (jnp.sum(pieces_ref[...].astype(F32), axis=0) * scale).astype(BF)
    out_ref[...] = jnp.broadcast_to(piece, out_ref.shape)


def sum_part(pieces, scale):
    return pl.pallas_call(
        functools.partial(sum_kernel, scale),
        out_shape=pltpu.VMEM(pieces.shape, BF),
        in_specs=[IN_VMEM],
        out_specs=IN_VMEM,
        compiler_params=params(4),
        cost_estimate=cost(1e6, 2e6),
        name="sum_part",
    )(pieces)


def order_kernel(*_):
    pass


def ordered(value, after):
    return pl.pallas_call(
        order_kernel,
        out_shape=jax.ShapeDtypeStruct(value.shape, value.dtype),
        in_specs=[ANYWHERE, ANYWHERE],
        out_specs=ANYWHERE,
        input_output_aliases={0: 0},
        compiler_params=params(1),
        name="ordered",
    )(value, after)


def result_kernel(side, half_ref, *refs):
    out_ref, block, sems = refs[-3:]
    core = lax.axis_index("core")
    lanes = pl.ds(pl.multiple_of((core if side == 0 else 1 - core) * LANES, LANES), LANES)
    copies = []
    for k in range(K):
        for part in range(2):
            block[k, part * LANES : (part + 1) * LANES, :] = half_ref[2 * k + part].astype(F32).T
        copies.append(pltpu.make_async_copy(block.at[k], out_ref.at[k, :, lanes], sems.at[k]))
        copies[k].start()
    for copy in copies:
        copy.wait()


def result_part(half, result=None):
    given = [] if result is None else [result]
    return pl.pallas_call(
        functools.partial(result_kernel, len(given)),
        out_shape=jax.ShapeDtypeStruct((K, C, C), F32),
        in_specs=[IN_VMEM] + [IN_HBM] * len(given),
        out_specs=IN_HBM,
        input_output_aliases={1: 0} if given else {},
        scratch_shapes=[pltpu.VMEM((K, C, LANES), F32), pltpu.SemaphoreType.DMA((K,))],
        compiler_params=params(6),
        cost_estimate=cost(1e6, 4e6),
        name="result_part",
    )(half, *given)


def extend(extended, n, row, left, right):
    extended[n] = jnp.concatenate([left, row, right], axis=0)


def grad_kernel(kept_ref, chip_ref, link_ref, left_ref, right_ref, weight_hbm, cot_hbm, _, out_ref, done_ref, weight, weight_turned, cot, extended, bands, cells, filtered, mixed, sems):
    core = lax.axis_index("core")
    cot_copy = pltpu.make_async_copy(cot_hbm, cot, sems.at[ROWS])
    cot_copy.start()
    weight_copy = pltpu.make_async_copy(weight_hbm, weight, sems.at[ROWS + 1])
    weight_copy.start()

    def fill(low, high):
        for n in range(2):
            extended[n] = low[n, 8 : 8 + EXT, :]
            extended[6 + n] = high[n, 8 : 8 + EXT, :]
            cells[n] = low[n, 2 * EDGE + NJ :, 0:LANES]
            cells[6 + n] = high[n, 2 * EDGE + NJ :, 0:LANES]

    pl.when(core == 0)(lambda: fill(link_ref, chip_ref))
    pl.when(core == 1)(lambda: fill(chip_ref, link_ref))
    for n in range(ROWS):
        cells[2 + n] = kept_ref[n]

    away = (TAPS - 1 - lax.broadcasted_iota(jnp.int32, (16, LANES), 1)) // WIDTH
    place = one_hot(lambda tap: (TAPS - 1 - tap) // WIDTH * EXT_WINDOW + 8 - RAD + (TAPS - 1 - tap) % WIDTH)
    lines = []
    for row in range(ROWS):
        taken = jnp.zeros((16, LANES), F32)
        for r in range(WIDTH):
            taken = jnp.where(away == r, cells[row + r].astype(F32), taken)
        lines.append(jnp.dot(taken.astype(BF), place, preferred_element_type=F32))
    cot_copy.wait()
    for n in range(ROWS):
        extend(extended, 2 + n, cot[n], left_ref[n, 8:, :], right_ref[n, :8, :])
    copies = [pltpu.make_async_copy(mixed.at[row], out_ref.at[row], sems.at[row]) for row in range(ROWS)]
    for row in range(ROWS):
        slot = row % 2
        for k in range(K):
            bands[slot, k * J : (k + 1) * J, :] = banded(lines[row][k : k + 1, :])[:, :DEPTH]
        for tile in range(STEPS):
            start = tile * J
            window = jnp.concatenate(
                [extended[row + r, start : start + EXT_WINDOW, :] for r in range(WIDTH)], axis=0
            )
            found = jnp.dot(bands[slot], window, preferred_element_type=F32).astype(BF)
            for k in range(K):
                filtered[slot, start : start + J, k * C : (k + 1) * C] = found[k * J : (k + 1) * J]
        if row == 0:
            weight_copy.wait()
            for k in range(K):
                columns = slice(k * C, (k + 1) * C)
                weight_turned[columns, :] = weight[columns, :].T
        mixed[row] = jnp.dot(filtered[slot], weight_turned[...], preferred_element_type=F32).astype(BF)
        copies[row].start()
    for copy in copies:
        copy.wait()
    done_ref[...] = jnp.zeros_like(done_ref)


def grad_part(kept, chip, link, left, right, weight, cotangent, after):
    return pl.pallas_call(
        grad_kernel,
        out_shape=(jax.ShapeDtypeStruct((ROWS, NJ, C), BF), pltpu.VMEM((8, LANES), F32)),
        in_specs=[IN_VMEM] * 5 + [IN_HBM, IN_HBM, ANYWHERE],
        out_specs=[IN_HBM, IN_VMEM],
        scratch_shapes=[
            pltpu.VMEM((K * C, C), BF),
            pltpu.VMEM((K * C, C), BF),
            pltpu.VMEM((ROWS, NJ, C), BF),
            pltpu.VMEM((PLACES, EXT, C), BF),
            pltpu.VMEM((2, K * J, DEPTH), BF),
            pltpu.VMEM((PLACES, 16, LANES), BF),
            pltpu.VMEM((2, NJ, K * C), BF),
            pltpu.VMEM((ROWS, NJ, C), BF),
            pltpu.SemaphoreType.DMA((ROWS + 2,)),
        ],
        compiler_params=params(20),
        cost_estimate=cost(8e9, 5e6),
        name="grad_input_part",
    )(kept, chip, link, left, right, in_hbm(weight), in_hbm(cotangent), after)


def shifted(block, axis, count, step, periodic):
    route = [(i, (i + step) % count) for i in range(count) if periodic or 0 <= i + step < count]
    return lax.ppermute(block, axis, route)


def per_device(features, basis, span_lo, span_hi, weight, cotangent):
    lat, chips = ("yz", "core"), ("yz", "lon")
    lats, lons = lax.axis_size("yz") * lax.axis_size("core"), lax.axis_size("lon")
    parts = lax.axis_size("yz") * lons
    swap = [(0, 1), (1, 0)]

    pairs = [(i, i + 1) for i in range(1, lats - 1, 2)]
    pairs = pairs + [(b, a) for a, b in pairs]
    chip, link = send_part(features)
    weight = weight.reshape(K * C, C)
    to_right, to_left, kept, turned, extended, bands = own_part(
        span_lo, span_hi, basis, cotangent, features, link
    )
    chip = lax.ppermute(chip, "core", swap)
    link = lax.ppermute(link, lat, pairs)
    near_left = shifted(to_right, "lon", lons, 1, True)
    near_right = shifted(to_left, "lon", lons, -1, True)
    total, near, weight_near = filter_part(0, chip, extended, bands, turned, weight)
    total, far, chip_cot, link_cot = filter_part(
        1, link, extended, bands, turned, total, kept, cotangent
    )
    own, other, chip_cot, link_cot = edge_part(near_left, near_right, total, near, far, chip_cot, link_cot)

    other = lax.ppermute(other, "core", swap)
    mixed, ends, to_right, to_left = mixed_part(near, far, weight_near)
    half = half_part(own, other, ends)
    pieces = lax.all_to_all(half.reshape(parts, -1, LANES), chips, 0, 0)
    link_cot = lax.ppermute(ordered(link_cot, half), lat, pairs)
    chip_cot = lax.ppermute(ordered(chip_cot, half), "core", swap)
    left = shifted(ordered(to_right, half), "lon", lons, 1, True)
    right = shifted(ordered(to_left, half), "lon", lons, -1, True)
    scale = 1.0 / math.sqrt(ROWS * lats * NJ * lons)
    copies = sum_part(pieces, scale)
    gathered = lax.all_to_all(copies, chips, 0, 0).reshape(PADDED_BLOCKS, LANES, LANES)
    mixed, mixed_done = ends_part(ends, left, right, mixed, copies)
    grad_input, grad_done = grad_part(
        kept, chip_cot, link_cot, near_left, near_right, weight, cotangent, mixed_done
    )
    gathered = ordered(gathered, grad_done)
    other = lax.ppermute(gathered, "core", swap)
    grad_weight = result_part(other, result_part(gathered))
    return mixed, grad_input, grad_weight


def solution(mesh):
    lats, lons = mesh.devices.shape
    split = Mesh(mesh.devices.reshape(lats // 2, 2, lons), ("yz", "core", "lon"))
    lat = ("yz", "core")
    return jax.shard_map(
        per_device,
        mesh=split,
        in_specs=(P(lat, "lon", None), P(lat, None, None), P(lat), P(lat), P(), P(lat, "lon", None)),
        out_specs=(P(lat, "lon", None), P(lat, "lon", None), P()),
        check_vma=False,
    )
```

```python
import functools
import math

import jax
import jax.numpy as jnp
from jax import lax
from jax.experimental import pallas as pl
from jax.experimental.pallas import tpu as pltpu
from jax.sharding import Mesh
from jax.sharding import PartitionSpec as P

K = 9
RAD = 2
WIDTH = 2 * RAD + 1
TAPS = WIDTH * WIDTH
ROWS = 4
PLACES = ROWS + 2 * RAD
NJ = 512
C = 256
J = 32
STEPS = NJ // J
EDGE = 16
EXT_WINDOW = 48
EXT = NJ + 16
DEPTH = WIDTH * EXT_WINDOW
WIDE = NJ + 2 * EDGE + 16
LANES = 128
BLOCKS = 2 * K
PADDED_BLOCKS = 20
MIB = 1024 * 1024
BF = jnp.bfloat16
F32 = jnp.float32

IN_VMEM = pl.BlockSpec(memory_space=pltpu.VMEM)
IN_SMEM = pl.BlockSpec(memory_space=pltpu.SMEM)
IN_HBM = pl.BlockSpec(memory_space=pltpu.HBM)
ANYWHERE = pl.BlockSpec(memory_space=pl.ANY)


def in_hbm(array):
    return pltpu.with_memory_space_constraint(array, pltpu.HBM)


def params(mib):
    return pltpu.CompilerParams(vmem_limit_bytes=mib * MIB)


def cost(flops, moved):
    return pl.CostEstimate(flops=int(flops), bytes_accessed=int(moved), transcendentals=0)


def banded(line):
    return pltpu.roll(jnp.broadcast_to(line, (J, 256)), 0, axis=1, stride=1, stride_axis=0).astype(BF)


def one_hot(lane_of_tap):
    tap = lax.broadcasted_iota(jnp.int32, (LANES, 256), 0)
    lane = lax.broadcasted_iota(jnp.int32, (LANES, 256), 1)
    return jnp.where((lane == lane_of_tap(tap)) & (tap < TAPS), 1.0, 0.0).astype(BF)


def send_kernel(feat_ref, chip_ref, link_ref, sems):
    core = lax.axis_index("core")
    copies = [
        pltpu.make_async_copy(feat_ref.at[pl.ds(first, 2)], ref, sems.at[n])
        for n, (ref, first) in enumerate(((link_ref, 2 * core), (chip_ref, 2 - 2 * core)))
    ]
    for copy in copies:
        copy.start()
    for copy in copies:
        copy.wait()


def send_part(features):
    return pl.pallas_call(
        send_kernel,
        out_shape=(pltpu.VMEM((2, NJ, C), BF), pltpu.VMEM((2, NJ, C), BF)),
        in_specs=[IN_HBM],
        out_specs=[IN_VMEM] * 2,
        scratch_shapes=[pltpu.SemaphoreType.DMA((2,))],
        compiler_params=params(2),
        cost_estimate=cost(0, 1e6),
        name="send_part",
    )(in_hbm(features))


def own_kernel(lo_ref, hi_ref, basis_ref, cot_ref, feat_ref, _, to_right_ref, to_left_ref, kept_ref, turned_ref, extended_ref, bands_ref, lo, hi, basis, cot, feat, sems):
    copies = (
        (lo_ref, lo),
        (hi_ref, hi),
        (basis_ref, basis),
        (cot_ref, cot),
        (feat_ref, feat),
    )
    copies = [pltpu.make_async_copy(a, b, sems.at[n]) for n, (a, b) in enumerate(copies)]
    for copy in copies:
        copy.start()
    place = one_hot(lambda tap: tap // WIDTH * EXT_WINDOW + 8 - RAD + tap % WIDTH)
    offset = lax.broadcasted_iota(jnp.int32, (16, LANES), 1) // WIDTH - RAD
    for copy in copies[:3]:
        copy.wait()
    for i in range(ROWS):
        cells = jnp.pad(basis[:, i, :], ((0, 16 - K), (0, LANES - TAPS)))
        cells = jnp.where((offset >= lo[i]) & (offset <= hi[i]), cells, jnp.zeros_like(cells)).astype(BF)
        kept_ref[i] = cells
        line = jnp.dot(cells, place, preferred_element_type=F32)
        for k in range(K):
            bands_ref[i, k * J : (k + 1) * J, :] = banded(line[k : k + 1, :])[:, :DEPTH]
    copies[3].wait()
    to_right_ref[...] = cot[:, NJ - EDGE :, :]
    to_left_ref[...] = cot[:, :EDGE, :]
    for pair in range(2):
        turned_ref[pair] = cot[2 * pair : 2 * pair + 2].reshape(2 * NJ, C).T
    copies[4].wait()
    gap = jnp.zeros((8, C), BF)
    for i in range(ROWS):
        extended_ref[i] = jnp.concatenate([gap, feat[i], gap], axis=0)


def own_part(span_lo, span_hi, basis, cotangent, features, after):
    basis = jnp.transpose(basis, (1, 0, 2))
    return pl.pallas_call(
        own_kernel,
        out_shape=(
            pltpu.VMEM((ROWS, EDGE, C), BF),
            pltpu.VMEM((ROWS, EDGE, C), BF),
            pltpu.VMEM((ROWS, 16, LANES), BF),
            pltpu.VMEM((2, C, 2 * NJ), BF),
            pltpu.VMEM((ROWS, EXT, C), BF),
            pltpu.VMEM((ROWS, K * J, DEPTH), BF),
        ),
        in_specs=[IN_HBM] * 5 + [ANYWHERE],
        out_specs=[IN_VMEM] * 6,
        scratch_shapes=[
            pltpu.SMEM((ROWS,), jnp.int32),
            pltpu.SMEM((ROWS,), jnp.int32),
            pltpu.VMEM(basis.shape, F32),
            pltpu.VMEM((ROWS, NJ, C), BF),
            pltpu.VMEM((ROWS, NJ, C), BF),
            pltpu.SemaphoreType.DMA((5,)),
        ],
        compiler_params=params(6),
        cost_estimate=cost(4e9, 4e6),
        name="own_part",
    )(*map(in_hbm, (span_lo, span_hi, basis, cotangent, features)), after)


def row_pair(side):
    core = lax.axis_index("core")
    return core if side == 0 else 1 - core


def filter_kernel(side, halo_ref, extended_ref, bands_ref, *refs):
    copies = []
    if side == 0:
        turned_ref, weight_hbm, total_ref, filtered, weight_ref, rows, sem = refs
        copies.append(pltpu.make_async_copy(weight_hbm, weight_ref, sem))
    else:
        turned_ref, before_ref, kept_ref, _, cot_ref, total_ref, filtered, chip_cot_ref, link_cot_ref, rows, kept, sems = refs
        core = lax.axis_index("core")
        for n, (ref, first) in enumerate(((chip_cot_ref, 2 - 2 * core), (link_cot_ref, 2 * core))):
            kept[n] = jnp.zeros((2, 16, C), BF)
            for i in range(2):
                kept[n, i, :, 0:LANES] = kept_ref[first + i]
            for source, start, size in ((cot_ref.at[pl.ds(first, 2)], EDGE, NJ), (kept.at[n], 2 * EDGE + NJ, 16)):
                target = ref.at[:, pl.ds(start, size)]
                copies.append(pltpu.make_async_copy(source, target, sems.at[len(copies)]))
    for copy in copies:
        copy.start()
    pair = row_pair(side)
    gap = jnp.zeros((8, C), BF)
    for n in range(2):
        rows[4 - 4 * pair + n] = jnp.concatenate([gap, halo_ref[n], gap], axis=0)
    for n in range(ROWS):
        rows[2 * pair + n] = extended_ref[n]
    middle = jnp.zeros((EXT_WINDOW - 16, C), BF)
    for row in range(2):
        bands = bands_ref[2 - 2 * pair + row]
        for tile in range(STEPS + 1):
            if tile < STEPS:
                start = tile * J
                first = row * NJ + start
                cells = [rows[row + r, start : start + EXT_WINDOW, :] for r in range(WIDTH)]
            else:
                first = 2 * NJ + row * J
                cells = []
                for r in range(WIDTH):
                    cells += [rows[row + r, NJ : NJ + 8, :], middle, rows[row + r, 8:16, :]]
            found = jnp.dot(bands, jnp.concatenate(cells, axis=0), preferred_element_type=F32).astype(BF)
            for k in range(K):
                filtered[first : first + J, k * C : (k + 1) * C] = found[k * J : (k + 1) * J]
    for k in range(K):
        columns = slice(k * C, (k + 1) * C)
        part = jnp.dot(turned_ref[1 - pair], filtered[0 : 2 * NJ, columns], preferred_element_type=F32)
        total_ref[:, columns] = part if side == 0 else before_ref[:, columns] + part
    for copy in copies:
        copy.wait()


def filter_part(side, *operands):
    outs = [pltpu.VMEM((C, K * C), F32), pltpu.VMEM((2 * (NJ + J), K * C), BF)]
    scratch = [pltpu.VMEM((6, EXT, C), BF)]
    if side == 0:
        outs += [pltpu.VMEM((K * C, C), BF)]
        scratch += [pltpu.SemaphoreType.DMA(())]
    else:
        outs += [pltpu.VMEM((2, WIDE, C), BF)] * 2
        scratch += [pltpu.VMEM((2, 2, 16, C), BF), pltpu.SemaphoreType.DMA((4,))]
    return pl.pallas_call(
        functools.partial(filter_kernel, side),
        out_shape=tuple(outs),
        in_specs=[IN_VMEM] * (len(operands) - 1) + [IN_HBM],
        out_specs=[IN_VMEM] * len(outs),
        scratch_shapes=scratch,
        compiler_params=params(8),
        cost_estimate=cost(1e8, 1e5),
        name="filter_part",
    )(*operands[:-1], in_hbm(operands[-1]))


def edge_kernel(left_ref, right_ref, total_ref, near_ref, far_ref, _, __, own_ref, other_ref, chip_cot_ref, link_cot_ref, sems):
    core = lax.axis_index("core")
    copies = []
    for ref, first in ((chip_cot_ref, 2 - 2 * core), (link_cot_ref, 2 * core)):
        for source, start in ((left_ref, 0), (right_ref, EDGE + NJ)):
            target = ref.at[:, pl.ds(start, EDGE)]
            copies.append(pltpu.make_async_copy(source.at[pl.ds(first, 2)], target, sems.at[len(copies)]))
    for copy in copies:
        copy.start()
    edges = []
    for side in range(2):
        for row in range(2):
            i = 2 - 2 * row_pair(side) + row
            edges += [right_ref[i], left_ref[i]]
    edges = jnp.concatenate(edges, axis=0).T
    for k in range(K):
        columns = slice(k * C, (k + 1) * C)
        beyond = jnp.concatenate([near_ref[2 * NJ :, columns], far_ref[2 * NJ :, columns]], axis=0)
        total = total_ref[:, columns] + jnp.dot(edges, beyond, preferred_element_type=F32)
        first, second = total[:LANES], total[LANES:]
        mine = jnp.where(core == 0, first, second)
        theirs = jnp.where(core == 0, second, first).astype(BF)
        for part in range(2):
            lanes = slice(part * LANES, (part + 1) * LANES)
            own_ref[2 * k + part] = mine[:, lanes]
            other_ref[2 * k + part] = theirs[:, lanes]
    for block in range(BLOCKS, PADDED_BLOCKS):
        own_ref[block] = jnp.zeros((LANES, LANES), F32)
        other_ref[block] = jnp.zeros((LANES, LANES), BF)
    for copy in copies:
        copy.wait()


def edge_part(left, right, total, near, far, chip_cot, link_cot):
    shape = (PADDED_BLOCKS, LANES, LANES)
    return pl.pallas_call(
        edge_kernel,
        out_shape=(
            pltpu.VMEM(shape, F32),
            pltpu.VMEM(shape, BF),
            pltpu.VMEM((2, WIDE, C), BF),
            pltpu.VMEM((2, WIDE, C), BF),
        ),
        in_specs=[IN_VMEM] * 5 + [ANYWHERE] * 2,
        out_specs=[IN_VMEM] * 2 + [ANYWHERE] * 2,
        input_output_aliases={5: 2, 6: 3},
        scratch_shapes=[pltpu.SemaphoreType.DMA((4,))],
        compiler_params=params(4),
        cost_estimate=cost(1e9, 4e6),
        name="edge_part",
    )(left, right, total, near, far, chip_cot, link_cot)


def half_kernel(own_ref, other_ref, _, out_ref, half, sems):
    copies = []
    for n in range(4):
        part = pl.ds(n * PADDED_BLOCKS // 4, PADDED_BLOCKS // 4)
        half[part] = (own_ref[part] + other_ref[part].astype(F32)).astype(BF)
        copies.append(pltpu.make_async_copy(half.at[part], out_ref.at[part], sems.at[n]))
        copies[n].start()
    for copy in copies:
        copy.wait()


def half_part(own, other, after):
    return pl.pallas_call(
        half_kernel,
        out_shape=jax.ShapeDtypeStruct(own.shape, BF),
        in_specs=[IN_VMEM] * 2 + [ANYWHERE],
        out_specs=IN_HBM,
        scratch_shapes=[pltpu.VMEM(own.shape, BF), pltpu.SemaphoreType.DMA((4,))],
        compiler_params=params(4),
        cost_estimate=cost(1e6, 3e6),
        name="half_part",
    )(own, other, after)


def mixed_kernel(side, filtered_ref, weight_ref, *refs):
    mixed_ref, ends_ref, to_right_ref, to_left_ref = refs[-4:]
    place = 2 * side
    if side == 1:
        to_right_ref[0:2] = refs[0][...]
        to_left_ref[0:2] = refs[1][...]
    beyond = jnp.dot(filtered_ref[2 * NJ :, :], weight_ref[...], preferred_element_type=F32)
    for row in range(2):
        to_right_ref[place + row] = beyond[row * J : row * J + EDGE]
        to_left_ref[place + row] = beyond[row * J + EDGE : (row + 1) * J]
        found = jnp.dot(
            filtered_ref[row * NJ : (row + 1) * NJ, :], weight_ref[...], preferred_element_type=F32
        )
        ends_ref[row, 0:EDGE, :] = found[0:EDGE]
        ends_ref[row, EDGE:, :] = found[NJ - EDGE :]
        mixed_ref[row] = found.astype(BF)


def mixed_part(side, *operands):
    return pl.pallas_call(
        functools.partial(mixed_kernel, side),
        out_shape=(
            pltpu.VMEM((2, NJ, C), BF),
            pltpu.VMEM((2, 2 * EDGE, C), F32),
            pltpu.VMEM((2 + 2 * side, EDGE, C), F32),
            pltpu.VMEM((2 + 2 * side, EDGE, C), F32),
        ),
        in_specs=[IN_VMEM] * len(operands),
        out_specs=[IN_VMEM] * 4,
        compiler_params=params(4),
        cost_estimate=cost(1e8, 1e5),
        name="mixed_part",
    )(*operands)


def ends_kernel(near_ends_ref, far_ends_ref, left_ref, right_ref, near_ref, far_ref, _, out_ref, done_ref, ends, sems):
    middle = pl.ds(EDGE, NJ - 2 * EDGE)
    copies = []
    for side, (ends_ref, mixed_ref) in enumerate(((near_ends_ref, near_ref), (far_ends_ref, far_ref))):
        rows = pl.ds(2 - 2 * row_pair(side), 2)
        places = slice(2 * side, 2 * side + 2)
        copies.append(pltpu.make_async_copy(mixed_ref.at[:, middle], out_ref.at[rows, middle], sems.at[side, 2]))
        copies[-1].start()
        ends[side, 0] = (ends_ref[:, 0:EDGE, :] + left_ref[places]).astype(BF)
        ends[side, 1] = (ends_ref[:, EDGE:, :] + right_ref[places]).astype(BF)
        for n, first in enumerate((0, NJ - EDGE)):
            target = out_ref.at[rows, pl.ds(first, EDGE)]
            copies.append(pltpu.make_async_copy(ends.at[side, n], target, sems.at[side, n]))
            copies[-1].start()
    done_ref[...] = jnp.zeros_like(done_ref)
    for copy in copies:
        copy.wait()


def ends_part(near_ends, far_ends, left, right, near, far, after):
    return pl.pallas_call(
        ends_kernel,
        out_shape=(jax.ShapeDtypeStruct((ROWS, NJ, C), BF), pltpu.VMEM((8, LANES), F32)),
        in_specs=[IN_VMEM] * 6 + [ANYWHERE],
        out_specs=[IN_HBM, IN_VMEM],
        scratch_shapes=[pltpu.VMEM((2, 2, 2, EDGE, C), BF), pltpu.SemaphoreType.DMA((2, 3))],
        compiler_params=params(4),
        cost_estimate=cost(1e6, 1e6),
        name="ends_part",
    )(near_ends, far_ends, left, right, near, far, after)


def sum_kernel(scale, pieces_ref, out_ref):
    piece = (jnp.sum(pieces_ref[...].astype(F32), axis=0) * scale).astype(BF)
    out_ref[...] = jnp.broadcast_to(piece, out_ref.shape)


def sum_part(pieces, scale):
    return pl.pallas_call(
        functools.partial(sum_kernel, scale),
        out_shape=pltpu.VMEM(pieces.shape, BF),
        in_specs=[IN_VMEM],
        out_specs=IN_VMEM,
        compiler_params=params(4),
        cost_estimate=cost(1e6, 2e6),
        name="sum_part",
    )(pieces)


def order_kernel(*_):
    pass


def ordered(value, after):
    return pl.pallas_call(
        order_kernel,
        out_shape=jax.ShapeDtypeStruct(value.shape, value.dtype),
        in_specs=[ANYWHERE, ANYWHERE],
        out_specs=ANYWHERE,
        input_output_aliases={0: 0},
        compiler_params=params(1),
        name="ordered",
    )(value, after)


def result_kernel(side, half_ref, *refs):
    out_ref, block, sems = refs[-3:]
    core = lax.axis_index("core")
    lanes = pl.ds(pl.multiple_of((core if side == 0 else 1 - core) * LANES, LANES), LANES)
    copies = []
    for k in range(K):
        for part in range(2):
            block[k, part * LANES : (part + 1) * LANES, :] = half_ref[2 * k + part].astype(F32).T
        copies.append(pltpu.make_async_copy(block.at[k], out_ref.at[k, :, lanes], sems.at[k]))
        copies[k].start()
    for copy in copies:
        copy.wait()


def result_part(half, result=None):
    given = [] if result is None else [result]
    return pl.pallas_call(
        functools.partial(result_kernel, len(given)),
        out_shape=jax.ShapeDtypeStruct((K, C, C), F32),
        in_specs=[IN_VMEM] + [IN_HBM] * len(given),
        out_specs=IN_HBM,
        input_output_aliases={1: 0} if given else {},
        scratch_shapes=[pltpu.VMEM((K, C, LANES), F32), pltpu.SemaphoreType.DMA((K,))],
        compiler_params=params(6),
        cost_estimate=cost(1e6, 4e6),
        name="result_part",
    )(half, *given)


def extend(extended, n, row, left, right):
    extended[n] = jnp.concatenate([left, row, right], axis=0)


def grad_kernel(kept_ref, chip_ref, link_ref, left_ref, right_ref, weight_hbm, cot_hbm, _, out_ref, done_ref, weight, weight_turned, cot, extended, bands, cells, filtered, mixed, sems):
    core = lax.axis_index("core")
    cot_copy = pltpu.make_async_copy(cot_hbm, cot, sems.at[ROWS])
    cot_copy.start()
    weight_copy = pltpu.make_async_copy(weight_hbm, weight, sems.at[ROWS + 1])
    weight_copy.start()

    def fill(low, high):
        for n in range(2):
            extended[n] = low[n, 8 : 8 + EXT, :]
            extended[6 + n] = high[n, 8 : 8 + EXT, :]
            cells[n] = low[n, 2 * EDGE + NJ :, 0:LANES]
            cells[6 + n] = high[n, 2 * EDGE + NJ :, 0:LANES]

    pl.when(core == 0)(lambda: fill(link_ref, chip_ref))
    pl.when(core == 1)(lambda: fill(chip_ref, link_ref))
    for n in range(ROWS):
        cells[2 + n] = kept_ref[n]

    away = (TAPS - 1 - lax.broadcasted_iota(jnp.int32, (16, LANES), 1)) // WIDTH
    place = one_hot(lambda tap: (TAPS - 1 - tap) // WIDTH * EXT_WINDOW + 8 - RAD + (TAPS - 1 - tap) % WIDTH)
    lines = []
    for row in range(ROWS):
        taken = jnp.zeros((16, LANES), F32)
        for r in range(WIDTH):
            taken = jnp.where(away == r, cells[row + r].astype(F32), taken)
        lines.append(jnp.dot(taken.astype(BF), place, preferred_element_type=F32))
    cot_copy.wait()
    for n in range(ROWS):
        extend(extended, 2 + n, cot[n], left_ref[n, 8:, :], right_ref[n, :8, :])
    copies = [pltpu.make_async_copy(mixed.at[row], out_ref.at[row], sems.at[row]) for row in range(ROWS)]
    for row in range(ROWS):
        slot = row % 2
        for k in range(K):
            bands[slot, k * J : (k + 1) * J, :] = banded(lines[row][k : k + 1, :])[:, :DEPTH]
        for tile in range(STEPS):
            start = tile * J
            window = jnp.concatenate(
                [extended[row + r, start : start + EXT_WINDOW, :] for r in range(WIDTH)], axis=0
            )
            found = jnp.dot(bands[slot], window, preferred_element_type=F32).astype(BF)
            for k in range(K):
                filtered[slot, start : start + J, k * C : (k + 1) * C] = found[k * J : (k + 1) * J]
        if row == 0:
            weight_copy.wait()
            for k in range(K):
                columns = slice(k * C, (k + 1) * C)
                weight_turned[columns, :] = weight[columns, :].T
        mixed[row] = jnp.dot(filtered[slot], weight_turned[...], preferred_element_type=F32).astype(BF)
        copies[row].start()
    for copy in copies:
        copy.wait()
    done_ref[...] = jnp.zeros_like(done_ref)


def grad_part(kept, chip, link, left, right, weight, cotangent, after):
    return pl.pallas_call(
        grad_kernel,
        out_shape=(jax.ShapeDtypeStruct((ROWS, NJ, C), BF), pltpu.VMEM((8, LANES), F32)),
        in_specs=[IN_VMEM] * 5 + [IN_HBM, IN_HBM, ANYWHERE],
        out_specs=[IN_HBM, IN_VMEM],
        scratch_shapes=[
            pltpu.VMEM((K * C, C), BF),
            pltpu.VMEM((K * C, C), BF),
            pltpu.VMEM((ROWS, NJ, C), BF),
            pltpu.VMEM((PLACES, EXT, C), BF),
            pltpu.VMEM((2, K * J, DEPTH), BF),
            pltpu.VMEM((PLACES, 16, LANES), BF),
            pltpu.VMEM((2, NJ, K * C), BF),
            pltpu.VMEM((ROWS, NJ, C), BF),
            pltpu.SemaphoreType.DMA((ROWS + 2,)),
        ],
        compiler_params=params(20),
        cost_estimate=cost(8e9, 5e6),
        name="grad_input_part",
    )(kept, chip, link, left, right, in_hbm(weight), in_hbm(cotangent), after)


def shifted(block, axis, count, step, periodic):
    route = [(i, (i + step) % count) for i in range(count) if periodic or 0 <= i + step < count]
    return lax.ppermute(block, axis, route)


def per_device(features, basis, span_lo, span_hi, weight, cotangent):
    lat, chips = ("yz", "core"), ("yz", "lon")
    lats, lons = lax.axis_size("yz") * lax.axis_size("core"), lax.axis_size("lon")
    parts = lax.axis_size("yz") * lons
    swap = [(0, 1), (1, 0)]

    pairs = [(i, i + 1) for i in range(1, lats - 1, 2)]
    pairs = pairs + [(b, a) for a, b in pairs]
    chip, link = send_part(features)
    weight = weight.reshape(K * C, C)
    to_right, to_left, kept, turned, extended, bands = own_part(
        span_lo, span_hi, basis, cotangent, features, link
    )
    chip = lax.ppermute(chip, "core", swap)
    link = lax.ppermute(link, lat, pairs)
    near_left = shifted(to_right, "lon", lons, 1, True)
    near_right = shifted(to_left, "lon", lons, -1, True)
    total, near, weight_near = filter_part(0, chip, extended, bands, turned, weight)
    near_mixed, near_ends, to_right, to_left = mixed_part(0, near, weight_near)
    total, far, chip_cot, link_cot = filter_part(
        1, link, extended, bands, turned, total, kept, to_right, cotangent
    )
    own, other, chip_cot, link_cot = edge_part(near_left, near_right, total, near, far, chip_cot, link_cot)

    other = lax.ppermute(other, "core", swap)
    far_mixed, far_ends, to_right, to_left = mixed_part(1, far, weight_near, to_right, to_left)
    half = half_part(own, other, far_ends)
    pieces = lax.all_to_all(half.reshape(parts, -1, LANES), chips, 0, 0)
    link_cot = lax.ppermute(ordered(link_cot, half), lat, pairs)
    chip_cot = lax.ppermute(ordered(chip_cot, half), "core", swap)
    left = shifted(ordered(to_right, half), "lon", lons, 1, True)
    right = shifted(ordered(to_left, half), "lon", lons, -1, True)
    scale = 1.0 / math.sqrt(ROWS * lats * NJ * lons)
    copies = sum_part(pieces, scale)
    gathered = lax.all_to_all(copies, chips, 0, 0).reshape(PADDED_BLOCKS, LANES, LANES)
    mixed, mixed_done = ends_part(near_ends, far_ends, left, right, near_mixed, far_mixed, copies)
    grad_input, grad_done = grad_part(
        kept, chip_cot, link_cot, near_left, near_right, weight, cotangent, mixed_done
    )
    gathered = ordered(gathered, grad_done)
    other = lax.ppermute(gathered, "core", swap)
    grad_weight = result_part(other, result_part(gathered))
    return mixed, grad_input, grad_weight


def solution(mesh):
    lats, lons = mesh.devices.shape
    split = Mesh(mesh.devices.reshape(lats // 2, 2, lons), ("yz", "core", "lon"))
    lat = ("yz", "core")
    return jax.shard_map(
        per_device,
        mesh=split,
        in_specs=(P(lat, "lon", None), P(lat, None, None), P(lat), P(lat), P(), P(lat, "lon", None)),
        out_specs=(P(lat, "lon", None), P(lat, "lon", None), P()),
        check_vma=False,
    )
```

```python
import functools
import math

import jax
import jax.numpy as jnp
from jax import lax
from jax.experimental import pallas as pl
from jax.experimental.pallas import tpu as pltpu
from jax.sharding import Mesh
from jax.sharding import PartitionSpec as P

K = 9
RAD = 2
WIDTH = 2 * RAD + 1
TAPS = WIDTH * WIDTH
ROWS = 4
PLACES = ROWS + 2 * RAD
NJ = 512
C = 256
J = 32
STEPS = NJ // J
EDGE = 16
EXT_WINDOW = 48
EXT = NJ + 16
DEPTH = WIDTH * EXT_WINDOW
WIDE = NJ + 2 * EDGE + 16
LANES = 128
BLOCKS = 2 * K
PADDED_BLOCKS = 20
MIB = 1024 * 1024
BF = jnp.bfloat16
F32 = jnp.float32

IN_VMEM = pl.BlockSpec(memory_space=pltpu.VMEM)
IN_HBM = pl.BlockSpec(memory_space=pltpu.HBM)
ANYWHERE = pl.BlockSpec(memory_space=pl.ANY)


def in_hbm(array):
    return pltpu.with_memory_space_constraint(array, pltpu.HBM)


def params(mib):
    return pltpu.CompilerParams(vmem_limit_bytes=mib * MIB)


def cost(flops, moved):
    return pl.CostEstimate(flops=int(flops), bytes_accessed=int(moved), transcendentals=0)


def banded(line):
    return pltpu.roll(jnp.broadcast_to(line, (J, 256)), 0, axis=1, stride=1, stride_axis=0).astype(BF)


def one_hot(lane_of_tap):
    tap = lax.broadcasted_iota(jnp.int32, (LANES, 256), 0)
    lane = lax.broadcasted_iota(jnp.int32, (LANES, 256), 1)
    return jnp.where((lane == lane_of_tap(tap)) & (tap < TAPS), 1.0, 0.0).astype(BF)


def send_kernel(feat_ref, chip_ref, link_ref, sems):
    core = lax.axis_index("core")
    copies = [
        pltpu.make_async_copy(feat_ref.at[pl.ds(first, 2)], ref, sems.at[n])
        for n, (ref, first) in enumerate(((link_ref, 2 * core), (chip_ref, 2 - 2 * core)))
    ]
    for copy in copies:
        copy.start()
    for copy in copies:
        copy.wait()


def send_part(features):
    return pl.pallas_call(
        send_kernel,
        out_shape=(pltpu.VMEM((2, NJ, C), BF), pltpu.VMEM((2, NJ, C), BF)),
        in_specs=[IN_HBM],
        out_specs=[IN_VMEM] * 2,
        scratch_shapes=[pltpu.SemaphoreType.DMA((2,))],
        compiler_params=params(2),
        cost_estimate=cost(0, 1e6),
        name="send_part",
    )(in_hbm(features))


def own_kernel(lo_ref, hi_ref, basis_ref, cot_ref, _, to_right_ref, to_left_ref, kept_ref, cot, bands_ref, lo, hi, basis, sems):
    copies = (
        (lo_ref, lo),
        (hi_ref, hi),
        (basis_ref, basis),
        (cot_ref, cot),
    )
    copies = [pltpu.make_async_copy(a, b, sems.at[n]) for n, (a, b) in enumerate(copies)]
    for copy in copies:
        copy.start()
    place = one_hot(lambda tap: tap // WIDTH * EXT_WINDOW + 8 - RAD + tap % WIDTH)
    offset = lax.broadcasted_iota(jnp.int32, (16, LANES), 1) // WIDTH - RAD
    for copy in copies[:3]:
        copy.wait()
    for i in range(ROWS):
        cells = jnp.pad(basis[:, i, :], ((0, 16 - K), (0, LANES - TAPS)))
        cells = jnp.where((offset >= lo[i]) & (offset <= hi[i]), cells, jnp.zeros_like(cells)).astype(BF)
        kept_ref[i] = cells
        line = jnp.dot(cells, place, preferred_element_type=F32)
        for k in range(K):
            bands_ref[i, k * J : (k + 1) * J, :] = banded(line[k : k + 1, :])[:, :DEPTH]
    for copy in copies[3:]:
        copy.wait()
    to_right_ref[...] = cot[:, NJ - EDGE :, :]
    to_left_ref[...] = cot[:, :EDGE, :]


def own_part(span_lo, span_hi, basis, cotangent, after):
    basis = jnp.transpose(basis, (1, 0, 2))
    return pl.pallas_call(
        own_kernel,
        out_shape=(
            pltpu.VMEM((ROWS, EDGE, C), BF),
            pltpu.VMEM((ROWS, EDGE, C), BF),
            pltpu.VMEM((ROWS, 16, LANES), BF),
            pltpu.VMEM((ROWS, NJ, C), BF),
            pltpu.VMEM((ROWS, K * J, DEPTH), BF),
        ),
        in_specs=[IN_HBM] * 4 + [ANYWHERE],
        out_specs=[IN_VMEM] * 5,
        scratch_shapes=[
            pltpu.SMEM((ROWS,), jnp.int32),
            pltpu.SMEM((ROWS,), jnp.int32),
            pltpu.VMEM(basis.shape, F32),
            pltpu.SemaphoreType.DMA((4,)),
        ],
        compiler_params=params(6),
        cost_estimate=cost(4e9, 4e6),
        name="own_part",
    )(*map(in_hbm, (span_lo, span_hi, basis, cotangent)), after)


def row_pair(side):
    core = lax.axis_index("core")
    return core if side == 0 else 1 - core


def filter_kernel(side, halo_ref, sent_chip_ref, sent_link_ref, bands_ref, near_cot_ref, *refs):
    copies = []
    if side == 0:
        weight_hbm, total_ref, filtered, weight_ref, rows, turned, sem = refs
        copies.append(pltpu.make_async_copy(weight_hbm, weight_ref, sem))
    else:
        before_ref, kept_ref, _, cot_ref, total_ref, filtered, chip_cot_ref, link_cot_ref, rows, turned, kept, sems = refs
        core = lax.axis_index("core")
        for n, (ref, first) in enumerate(((chip_cot_ref, 2 - 2 * core), (link_cot_ref, 2 * core))):
            kept[n] = jnp.zeros((2, 16, C), BF)
            for i in range(2):
                kept[n, i, :, 0:LANES] = kept_ref[first + i]
            for source, start, size in ((cot_ref.at[pl.ds(first, 2)], EDGE, NJ), (kept.at[n], 2 * EDGE + NJ, 16)):
                target = ref.at[:, pl.ds(start, size)]
                copies.append(pltpu.make_async_copy(source, target, sems.at[len(copies)]))
    for copy in copies:
        copy.start()
    pair = row_pair(side)
    gap = jnp.zeros((8, C), BF)
    for n in range(2):
        rows[4 - 4 * pair + n] = jnp.concatenate([gap, halo_ref[n], gap], axis=0)
    own_core = lax.axis_index("core")
    for n in range(2):
        rows[2 * pair + 2 * own_core + n] = jnp.concatenate([gap, sent_link_ref[n], gap], axis=0)
        rows[2 * pair + 2 - 2 * own_core + n] = jnp.concatenate([gap, sent_chip_ref[n], gap], axis=0)
    turned[...] = near_cot_ref[pl.ds(2 - 2 * pair, 2)].reshape(2 * NJ, C).T
    middle = jnp.zeros((EXT_WINDOW - 16, C), BF)
    for row in range(2):
        bands = bands_ref[2 - 2 * pair + row]
        for tile in range(STEPS + 1):
            if tile < STEPS:
                start = tile * J
                first = row * NJ + start
                cells = [rows[row + r, start : start + EXT_WINDOW, :] for r in range(WIDTH)]
            else:
                first = 2 * NJ + row * J
                cells = []
                for r in range(WIDTH):
                    cells += [rows[row + r, NJ : NJ + 8, :], middle, rows[row + r, 8:16, :]]
            found = jnp.dot(bands, jnp.concatenate(cells, axis=0), preferred_element_type=F32).astype(BF)
            for k in range(K):
                filtered[first : first + J, k * C : (k + 1) * C] = found[k * J : (k + 1) * J]
    for k in range(K):
        columns = slice(k * C, (k + 1) * C)
        part = jnp.dot(turned[...], filtered[0 : 2 * NJ, columns], preferred_element_type=F32)
        total_ref[:, columns] = part if side == 0 else before_ref[:, columns] + part
    for copy in copies:
        copy.wait()


def filter_part(side, *operands):
    outs = [pltpu.VMEM((C, K * C), F32), pltpu.VMEM((2 * (NJ + J), K * C), BF)]
    scratch = [pltpu.VMEM((6, EXT, C), BF), pltpu.VMEM((C, 2 * NJ), BF)]
    if side == 0:
        outs += [pltpu.VMEM((K * C, C), BF)]
        scratch += [pltpu.SemaphoreType.DMA(())]
    else:
        outs += [pltpu.VMEM((2, WIDE, C), BF)] * 2
        scratch += [pltpu.VMEM((2, 2, 16, C), BF), pltpu.SemaphoreType.DMA((4,))]
    return pl.pallas_call(
        functools.partial(filter_kernel, side),
        out_shape=tuple(outs),
        in_specs=[IN_VMEM] * (len(operands) - 1) + [IN_HBM],
        out_specs=[IN_VMEM] * len(outs),
        scratch_shapes=scratch,
        compiler_params=params(8),
        cost_estimate=cost(1e8, 1e5),
        name="filter_part",
    )(*operands[:-1], in_hbm(operands[-1]))


def edge_kernel(left_ref, right_ref, total_ref, near_ref, far_ref, _, __, own_ref, other_ref, chip_cot_ref, link_cot_ref, sems):
    core = lax.axis_index("core")
    copies = []
    for ref, first in ((chip_cot_ref, 2 - 2 * core), (link_cot_ref, 2 * core)):
        for source, start in ((left_ref, 0), (right_ref, EDGE + NJ)):
            target = ref.at[:, pl.ds(start, EDGE)]
            copies.append(pltpu.make_async_copy(source.at[pl.ds(first, 2)], target, sems.at[len(copies)]))
    for copy in copies:
        copy.start()
    edges = []
    for side in range(2):
        for row in range(2):
            i = 2 - 2 * row_pair(side) + row
            edges += [right_ref[i], left_ref[i]]
    edges = jnp.concatenate(edges, axis=0).T
    for k in range(K):
        columns = slice(k * C, (k + 1) * C)
        beyond = jnp.concatenate([near_ref[2 * NJ :, columns], far_ref[2 * NJ :, columns]], axis=0)
        total = total_ref[:, columns] + jnp.dot(edges, beyond, preferred_element_type=F32)
        first, second = total[:LANES], total[LANES:]
        mine = jnp.where(core == 0, first, second)
        theirs = jnp.where(core == 0, second, first).astype(BF)
        for part in range(2):
            lanes = slice(part * LANES, (part + 1) * LANES)
            own_ref[2 * k + part] = mine[:, lanes]
            other_ref[2 * k + part] = theirs[:, lanes]
    for block in range(BLOCKS, PADDED_BLOCKS):
        own_ref[block] = jnp.zeros((LANES, LANES), F32)
        other_ref[block] = jnp.zeros((LANES, LANES), BF)
    for copy in copies:
        copy.wait()


def edge_part(left, right, total, near, far, chip_cot, link_cot):
    shape = (PADDED_BLOCKS, LANES, LANES)
    return pl.pallas_call(
        edge_kernel,
        out_shape=(
            pltpu.VMEM(shape, F32),
            pltpu.VMEM(shape, BF),
            pltpu.VMEM((2, WIDE, C), BF),
            pltpu.VMEM((2, WIDE, C), BF),
        ),
        in_specs=[IN_VMEM] * 5 + [ANYWHERE] * 2,
        out_specs=[IN_VMEM] * 2 + [ANYWHERE] * 2,
        input_output_aliases={5: 2, 6: 3},
        scratch_shapes=[pltpu.SemaphoreType.DMA((4,))],
        compiler_params=params(4),
        cost_estimate=cost(1e9, 4e6),
        name="edge_part",
    )(left, right, total, near, far, chip_cot, link_cot)


def half_kernel(own_ref, other_ref, _, out_ref, half, sems):
    copies = []
    for n in range(4):
        part = pl.ds(n * PADDED_BLOCKS // 4, PADDED_BLOCKS // 4)
        half[part] = (own_ref[part] + other_ref[part].astype(F32)).astype(BF)
        copies.append(pltpu.make_async_copy(half.at[part], out_ref.at[part], sems.at[n]))
        copies[n].start()
    for copy in copies:
        copy.wait()


def half_part(own, other, after):
    return pl.pallas_call(
        half_kernel,
        out_shape=jax.ShapeDtypeStruct(own.shape, BF),
        in_specs=[IN_VMEM] * 2 + [ANYWHERE],
        out_specs=IN_HBM,
        scratch_shapes=[pltpu.VMEM(own.shape, BF), pltpu.SemaphoreType.DMA((4,))],
        compiler_params=params(4),
        cost_estimate=cost(1e6, 3e6),
        name="half_part",
    )(own, other, after)


def mixed_kernel(side, filtered_ref, weight_ref, *refs):
    mixed_ref, ends_ref, to_right_ref, to_left_ref = refs[-4:]
    place = 2 * side
    if side == 1:
        to_right_ref[0:2] = refs[0][...]
        to_left_ref[0:2] = refs[1][...]
    beyond = jnp.dot(filtered_ref[2 * NJ :, :], weight_ref[...], preferred_element_type=F32)
    for row in range(2):
        to_right_ref[place + row] = beyond[row * J : row * J + EDGE]
        to_left_ref[place + row] = beyond[row * J + EDGE : (row + 1) * J]
        found = jnp.dot(
            filtered_ref[row * NJ : (row + 1) * NJ, :], weight_ref[...], preferred_element_type=F32
        )
        ends_ref[row, 0:EDGE, :] = found[0:EDGE]
        ends_ref[row, EDGE:, :] = found[NJ - EDGE :]
        mixed_ref[row] = found.astype(BF)


def mixed_part(side, *operands):
    return pl.pallas_call(
        functools.partial(mixed_kernel, side),
        out_shape=(
            pltpu.VMEM((2, NJ, C), BF),
            pltpu.VMEM((2, 2 * EDGE, C), F32),
            pltpu.VMEM((2 + 2 * side, EDGE, C), F32),
            pltpu.VMEM((2 + 2 * side, EDGE, C), F32),
        ),
        in_specs=[IN_VMEM] * len(operands),
        out_specs=[IN_VMEM] * 4,
        compiler_params=params(4),
        cost_estimate=cost(1e8, 1e5),
        name="mixed_part",
    )(*operands)


def ends_kernel(near_ends_ref, far_ends_ref, left_ref, right_ref, near_ref, far_ref, _, out_ref, done_ref, ends, sems):
    middle = pl.ds(EDGE, NJ - 2 * EDGE)
    copies = []
    for side, (ends_ref, mixed_ref) in enumerate(((near_ends_ref, near_ref), (far_ends_ref, far_ref))):
        rows = pl.ds(2 - 2 * row_pair(side), 2)
        places = slice(2 * side, 2 * side + 2)
        copies.append(pltpu.make_async_copy(mixed_ref.at[:, middle], out_ref.at[rows, middle], sems.at[side, 2]))
        copies[-1].start()
        ends[side, 0] = (ends_ref[:, 0:EDGE, :] + left_ref[places]).astype(BF)
        ends[side, 1] = (ends_ref[:, EDGE:, :] + right_ref[places]).astype(BF)
        for n, first in enumerate((0, NJ - EDGE)):
            target = out_ref.at[rows, pl.ds(first, EDGE)]
            copies.append(pltpu.make_async_copy(ends.at[side, n], target, sems.at[side, n]))
            copies[-1].start()
    done_ref[...] = jnp.zeros_like(done_ref)
    for copy in copies:
        copy.wait()


def ends_part(near_ends, far_ends, left, right, near, far, after):
    return pl.pallas_call(
        ends_kernel,
        out_shape=(jax.ShapeDtypeStruct((ROWS, NJ, C), BF), pltpu.VMEM((8, LANES), F32)),
        in_specs=[IN_VMEM] * 6 + [ANYWHERE],
        out_specs=[IN_HBM, IN_VMEM],
        scratch_shapes=[pltpu.VMEM((2, 2, 2, EDGE, C), BF), pltpu.SemaphoreType.DMA((2, 3))],
        compiler_params=params(4),
        cost_estimate=cost(1e6, 1e6),
        name="ends_part",
    )(near_ends, far_ends, left, right, near, far, after)


def sum_kernel(scale, pieces_ref, out_ref):
    piece = (jnp.sum(pieces_ref[...].astype(F32), axis=0) * scale).astype(BF)
    out_ref[...] = jnp.broadcast_to(piece, out_ref.shape)


def sum_part(pieces, scale):
    return pl.pallas_call(
        functools.partial(sum_kernel, scale),
        out_shape=pltpu.VMEM(pieces.shape, BF),
        in_specs=[IN_VMEM],
        out_specs=IN_VMEM,
        compiler_params=params(4),
        cost_estimate=cost(1e6, 2e6),
        name="sum_part",
    )(pieces)


def order_kernel(*_):
    pass


def ordered(value, after):
    return pl.pallas_call(
        order_kernel,
        out_shape=jax.ShapeDtypeStruct(value.shape, value.dtype),
        in_specs=[ANYWHERE, ANYWHERE],
        out_specs=ANYWHERE,
        input_output_aliases={0: 0},
        compiler_params=params(1),
        name="ordered",
    )(value, after)


def result_kernel(side, half_ref, *refs):
    out_ref, block, sems = refs[-3:]
    core = lax.axis_index("core")
    lanes = pl.ds(pl.multiple_of((core if side == 0 else 1 - core) * LANES, LANES), LANES)
    copies = []
    for k in range(K):
        for part in range(2):
            block[k, part * LANES : (part + 1) * LANES, :] = half_ref[2 * k + part].astype(F32).T
        copies.append(pltpu.make_async_copy(block.at[k], out_ref.at[k, :, lanes], sems.at[k]))
        copies[k].start()
    for copy in copies:
        copy.wait()


def result_part(half, result=None):
    given = [] if result is None else [result]
    return pl.pallas_call(
        functools.partial(result_kernel, len(given)),
        out_shape=jax.ShapeDtypeStruct((K, C, C), F32),
        in_specs=[IN_VMEM] + [IN_HBM] * len(given),
        out_specs=IN_HBM,
        input_output_aliases={1: 0} if given else {},
        scratch_shapes=[pltpu.VMEM((K, C, LANES), F32), pltpu.SemaphoreType.DMA((K,))],
        compiler_params=params(6),
        cost_estimate=cost(1e6, 4e6),
        name="result_part",
    )(half, *given)


def extend(extended, n, row, left, right):
    extended[n] = jnp.concatenate([left, row, right], axis=0)


def grad_kernel(kept_ref, chip_ref, link_ref, left_ref, right_ref, weight_hbm, cot_hbm, _, out_ref, done_ref, weight, weight_turned, cot, extended, bands, cells, filtered, mixed, sems):
    core = lax.axis_index("core")
    cot_copy = pltpu.make_async_copy(cot_hbm, cot, sems.at[ROWS])
    cot_copy.start()
    weight_copy = pltpu.make_async_copy(weight_hbm, weight, sems.at[ROWS + 1])
    weight_copy.start()

    def fill(low, high):
        for n in range(2):
            extended[n] = low[n, 8 : 8 + EXT, :]
            extended[6 + n] = high[n, 8 : 8 + EXT, :]
            cells[n] = low[n, 2 * EDGE + NJ :, 0:LANES]
            cells[6 + n] = high[n, 2 * EDGE + NJ :, 0:LANES]

    pl.when(core == 0)(lambda: fill(link_ref, chip_ref))
    pl.when(core == 1)(lambda: fill(chip_ref, link_ref))
    for n in range(ROWS):
        cells[2 + n] = kept_ref[n]

    away = (TAPS - 1 - lax.broadcasted_iota(jnp.int32, (16, LANES), 1)) // WIDTH
    place = one_hot(lambda tap: (TAPS - 1 - tap) // WIDTH * EXT_WINDOW + 8 - RAD + (TAPS - 1 - tap) % WIDTH)
    lines = []
    for row in range(ROWS):
        taken = jnp.zeros((16, LANES), F32)
        for r in range(WIDTH):
            taken = jnp.where(away == r, cells[row + r].astype(F32), taken)
        lines.append(jnp.dot(taken.astype(BF), place, preferred_element_type=F32))
    cot_copy.wait()
    for n in range(ROWS):
        extend(extended, 2 + n, cot[n], left_ref[n, 8:, :], right_ref[n, :8, :])
    copies = [pltpu.make_async_copy(mixed.at[row], out_ref.at[row], sems.at[row]) for row in range(ROWS)]
    for row in range(ROWS):
        slot = row % 2
        for k in range(K):
            bands[slot, k * J : (k + 1) * J, :] = banded(lines[row][k : k + 1, :])[:, :DEPTH]
        for tile in range(STEPS):
            start = tile * J
            window = jnp.concatenate(
                [extended[row + r, start : start + EXT_WINDOW, :] for r in range(WIDTH)], axis=0
            )
            found = jnp.dot(bands[slot], window, preferred_element_type=F32).astype(BF)
            for k in range(K):
                filtered[slot, start : start + J, k * C : (k + 1) * C] = found[k * J : (k + 1) * J]
        if row == 0:
            weight_copy.wait()
            for k in range(K):
                columns = slice(k * C, (k + 1) * C)
                weight_turned[columns, :] = weight[columns, :].T
        mixed[row] = jnp.dot(filtered[slot], weight_turned[...], preferred_element_type=F32).astype(BF)
        copies[row].start()
    for copy in copies:
        copy.wait()
    done_ref[...] = jnp.zeros_like(done_ref)


def grad_part(kept, chip, link, left, right, weight, cotangent, after):
    return pl.pallas_call(
        grad_kernel,
        out_shape=(jax.ShapeDtypeStruct((ROWS, NJ, C), BF), pltpu.VMEM((8, LANES), F32)),
        in_specs=[IN_VMEM] * 5 + [IN_HBM, IN_HBM, ANYWHERE],
        out_specs=[IN_HBM, IN_VMEM],
        scratch_shapes=[
            pltpu.VMEM((K * C, C), BF),
            pltpu.VMEM((K * C, C), BF),
            pltpu.VMEM((ROWS, NJ, C), BF),
            pltpu.VMEM((PLACES, EXT, C), BF),
            pltpu.VMEM((2, K * J, DEPTH), BF),
            pltpu.VMEM((PLACES, 16, LANES), BF),
            pltpu.VMEM((2, NJ, K * C), BF),
            pltpu.VMEM((ROWS, NJ, C), BF),
            pltpu.SemaphoreType.DMA((ROWS + 2,)),
        ],
        compiler_params=params(20),
        cost_estimate=cost(8e9, 5e6),
        name="grad_input_part",
    )(kept, chip, link, left, right, in_hbm(weight), in_hbm(cotangent), after)


def shifted(block, axis, count, step, periodic):
    route = [(i, (i + step) % count) for i in range(count) if periodic or 0 <= i + step < count]
    return lax.ppermute(block, axis, route)


def per_device(features, basis, span_lo, span_hi, weight, cotangent):
    lat, chips = ("yz", "core"), ("yz", "lon")
    lats, lons = lax.axis_size("yz") * lax.axis_size("core"), lax.axis_size("lon")
    parts = lax.axis_size("yz") * lons
    swap = [(0, 1), (1, 0)]

    pairs = [(i, i + 1) for i in range(1, lats - 1, 2)]
    pairs = pairs + [(b, a) for a, b in pairs]
    sent_chip, sent_link = send_part(features)
    weight = weight.reshape(K * C, C)
    to_right, to_left, kept, near_cot, bands = own_part(
        span_lo, span_hi, basis, cotangent, sent_link
    )
    chip = lax.ppermute(sent_chip, "core", swap)
    link = lax.ppermute(sent_link, lat, pairs)
    near_left = shifted(to_right, "lon", lons, 1, True)
    near_right = shifted(to_left, "lon", lons, -1, True)
    total, near, weight_near = filter_part(0, chip, sent_chip, sent_link, bands, near_cot, weight)
    near_mixed, near_ends, to_right, to_left = mixed_part(0, near, weight_near)
    total, far, chip_cot, link_cot = filter_part(
        1, link, sent_chip, sent_link, bands, near_cot, total, kept, to_right, cotangent
    )
    own, other, chip_cot, link_cot = edge_part(near_left, near_right, total, near, far, chip_cot, link_cot)

    other = lax.ppermute(other, "core", swap)
    far_mixed, far_ends, to_right, to_left = mixed_part(1, far, weight_near, to_right, to_left)
    half = half_part(own, other, far_ends)
    pieces = lax.all_to_all(half.reshape(parts, -1, LANES), chips, 0, 0)
    link_cot = lax.ppermute(ordered(link_cot, half), lat, pairs)
    chip_cot = lax.ppermute(ordered(chip_cot, half), "core", swap)
    left = shifted(ordered(to_right, half), "lon", lons, 1, True)
    right = shifted(ordered(to_left, half), "lon", lons, -1, True)
    scale = 1.0 / math.sqrt(ROWS * lats * NJ * lons)
    copies = sum_part(pieces, scale)
    gathered = lax.all_to_all(copies, chips, 0, 0).reshape(PADDED_BLOCKS, LANES, LANES)
    mixed, mixed_done = ends_part(near_ends, far_ends, left, right, near_mixed, far_mixed, copies)
    grad_input, grad_done = grad_part(
        kept, chip_cot, link_cot, near_left, near_right, weight, cotangent, mixed_done
    )
    gathered = ordered(gathered, grad_done)
    other = lax.ppermute(gathered, "core", swap)
    grad_weight = result_part(other, result_part(gathered))
    return mixed, grad_input, grad_weight


def solution(mesh):
    lats, lons = mesh.devices.shape
    split = Mesh(mesh.devices.reshape(lats // 2, 2, lons), ("yz", "core", "lon"))
    lat = ("yz", "core")
    return jax.shard_map(
        per_device,
        mesh=split,
        in_specs=(P(lat, "lon", None), P(lat, None, None), P(lat), P(lat), P(), P(lat, "lon", None)),
        out_specs=(P(lat, "lon", None), P(lat, "lon", None), P()),
        check_vma=False,
    )
```

```python
import functools
import math

import jax
import jax.numpy as jnp
from jax import lax
from jax.experimental import pallas as pl
from jax.experimental.pallas import tpu as pltpu
from jax.sharding import Mesh
from jax.sharding import PartitionSpec as P

K = 9
RAD = 2
WIDTH = 2 * RAD + 1
TAPS = WIDTH * WIDTH
ROWS = 4
PLACES = ROWS + 2 * RAD
NJ = 512
C = 256
J = 32
STEPS = NJ // J
EDGE = 16
EXT_WINDOW = 48
EXT = NJ + 16
DEPTH = WIDTH * EXT_WINDOW
WIDE = NJ + 2 * EDGE + 16
LANES = 128
BLOCKS = 2 * K
PADDED_BLOCKS = 20
MIB = 1024 * 1024
BF = jnp.bfloat16
F32 = jnp.float32

IN_VMEM = pl.BlockSpec(memory_space=pltpu.VMEM)
IN_HBM = pl.BlockSpec(memory_space=pltpu.HBM)
ANYWHERE = pl.BlockSpec(memory_space=pl.ANY)


def in_hbm(array):
    return pltpu.with_memory_space_constraint(array, pltpu.HBM)


def params(mib):
    return pltpu.CompilerParams(vmem_limit_bytes=mib * MIB)


def cost(flops, moved):
    return pl.CostEstimate(flops=int(flops), bytes_accessed=int(moved), transcendentals=0)


def banded(line):
    return pltpu.roll(jnp.broadcast_to(line, (J, 256)), 0, axis=1, stride=1, stride_axis=0).astype(BF)


def one_hot(lane_of_tap):
    tap = lax.broadcasted_iota(jnp.int32, (LANES, 256), 0)
    lane = lax.broadcasted_iota(jnp.int32, (LANES, 256), 1)
    return jnp.where((lane == lane_of_tap(tap)) & (tap < TAPS), 1.0, 0.0).astype(BF)


def send_kernel(feat_ref, chip_ref, link_ref, sems):
    core = lax.axis_index("core")
    copies = [
        pltpu.make_async_copy(feat_ref.at[pl.ds(first, 2)], ref, sems.at[n])
        for n, (ref, first) in enumerate(((link_ref, 2 * core), (chip_ref, 2 - 2 * core)))
    ]
    for copy in copies:
        copy.start()
    for copy in copies:
        copy.wait()


def send_part(features):
    return pl.pallas_call(
        send_kernel,
        out_shape=(pltpu.VMEM((2, NJ, C), BF), pltpu.VMEM((2, NJ, C), BF)),
        in_specs=[IN_HBM],
        out_specs=[IN_VMEM] * 2,
        scratch_shapes=[pltpu.SemaphoreType.DMA((2,))],
        compiler_params=params(2),
        cost_estimate=cost(0, 1e6),
        name="send_part",
    )(in_hbm(features))


def own_kernel(lo_ref, hi_ref, basis_ref, cot_ref, _, to_right_ref, to_left_ref, kept_ref, bands_ref, lo, hi, basis, sems):
    copies = (
        (lo_ref, lo),
        (hi_ref, hi),
        (basis_ref, basis),
        (cot_ref.at[:, pl.ds(NJ - EDGE, EDGE)], to_right_ref),
        (cot_ref.at[:, pl.ds(0, EDGE)], to_left_ref),
    )
    copies = [pltpu.make_async_copy(a, b, sems.at[n]) for n, (a, b) in enumerate(copies)]
    for copy in copies:
        copy.start()
    place = one_hot(lambda tap: tap // WIDTH * EXT_WINDOW + 8 - RAD + tap % WIDTH)
    offset = lax.broadcasted_iota(jnp.int32, (16, LANES), 1) // WIDTH - RAD
    for copy in copies[:3]:
        copy.wait()
    for i in range(ROWS):
        cells = jnp.pad(basis[:, i, :], ((0, 16 - K), (0, LANES - TAPS)))
        cells = jnp.where((offset >= lo[i]) & (offset <= hi[i]), cells, jnp.zeros_like(cells)).astype(BF)
        kept_ref[i] = cells
        line = jnp.dot(cells, place, preferred_element_type=F32)
        for k in range(K):
            bands_ref[i, k * J : (k + 1) * J, :] = banded(line[k : k + 1, :])[:, :DEPTH]
    for copy in copies[3:]:
        copy.wait()


def own_part(span_lo, span_hi, basis, cotangent, after):
    basis = jnp.transpose(basis, (1, 0, 2))
    return pl.pallas_call(
        own_kernel,
        out_shape=(
            pltpu.VMEM((ROWS, EDGE, C), BF),
            pltpu.VMEM((ROWS, EDGE, C), BF),
            pltpu.VMEM((ROWS, 16, LANES), BF),
            pltpu.VMEM((ROWS, K * J, DEPTH), BF),
        ),
        in_specs=[IN_HBM] * 4 + [ANYWHERE],
        out_specs=[IN_VMEM] * 4,
        scratch_shapes=[
            pltpu.SMEM((ROWS,), jnp.int32),
            pltpu.SMEM((ROWS,), jnp.int32),
            pltpu.VMEM(basis.shape, F32),
            pltpu.SemaphoreType.DMA((5,)),
        ],
        compiler_params=params(6),
        cost_estimate=cost(4e9, 4e6),
        name="own_part",
    )(*map(in_hbm, (span_lo, span_hi, basis, cotangent)), after)


def row_pair(side):
    core = lax.axis_index("core")
    return core if side == 0 else 1 - core


def filter_kernel(side, halo_ref, sent_chip_ref, sent_link_ref, bands_ref, near_cot_ref, *refs):
    copies = []
    if side == 0:
        weight_hbm, total_ref, filtered, weight_ref, rows, turned, sem = refs
        copies.append(pltpu.make_async_copy(weight_hbm, weight_ref, sem))
    else:
        before_ref, kept_ref, _, cot_ref, total_ref, filtered, chip_cot_ref, link_cot_ref, rows, turned, kept, sems = refs
        core = lax.axis_index("core")
        for n, (ref, first) in enumerate(((chip_cot_ref, 2 - 2 * core), (link_cot_ref, 2 * core))):
            kept[n] = jnp.zeros((2, 16, C), BF)
            for i in range(2):
                kept[n, i, :, 0:LANES] = kept_ref[first + i]
            for source, start, size in ((cot_ref.at[pl.ds(first, 2)], EDGE, NJ), (kept.at[n], 2 * EDGE + NJ, 16)):
                target = ref.at[:, pl.ds(start, size)]
                copies.append(pltpu.make_async_copy(source, target, sems.at[len(copies)]))
    for copy in copies:
        copy.start()
    pair = row_pair(side)
    gap = jnp.zeros((8, C), BF)
    for n in range(2):
        rows[4 - 4 * pair + n] = jnp.concatenate([gap, halo_ref[n], gap], axis=0)
    own_core = lax.axis_index("core")
    for n in range(2):
        rows[2 * pair + 2 * own_core + n] = jnp.concatenate([gap, sent_link_ref[n], gap], axis=0)
        rows[2 * pair + 2 - 2 * own_core + n] = jnp.concatenate([gap, sent_chip_ref[n], gap], axis=0)
    turned[...] = near_cot_ref[pl.ds(2 - 2 * pair, 2)].reshape(2 * NJ, C).T
    middle = jnp.zeros((EXT_WINDOW - 16, C), BF)
    for row in range(2):
        bands = bands_ref[2 - 2 * pair + row]
        for tile in range(STEPS + 1):
            if tile < STEPS:
                start = tile * J
                first = row * NJ + start
                cells = [rows[row + r, start : start + EXT_WINDOW, :] for r in range(WIDTH)]
            else:
                first = 2 * NJ + row * J
                cells = []
                for r in range(WIDTH):
                    cells += [rows[row + r, NJ : NJ + 8, :], middle, rows[row + r, 8:16, :]]
            found = jnp.dot(bands, jnp.concatenate(cells, axis=0), preferred_element_type=F32).astype(BF)
            for k in range(K):
                filtered[first : first + J, k * C : (k + 1) * C] = found[k * J : (k + 1) * J]
    for k in range(K):
        columns = slice(k * C, (k + 1) * C)
        part = jnp.dot(turned[...], filtered[0 : 2 * NJ, columns], preferred_element_type=F32)
        total_ref[:, columns] = part if side == 0 else before_ref[:, columns] + part
    for copy in copies:
        copy.wait()


def filter_part(side, *operands):
    outs = [pltpu.VMEM((C, K * C), F32), pltpu.VMEM((2 * (NJ + J), K * C), BF)]
    scratch = [pltpu.VMEM((6, EXT, C), BF), pltpu.VMEM((C, 2 * NJ), BF)]
    if side == 0:
        outs += [pltpu.VMEM((K * C, C), BF)]
        scratch += [pltpu.SemaphoreType.DMA(())]
    else:
        outs += [pltpu.VMEM((2, WIDE, C), BF)] * 2
        scratch += [pltpu.VMEM((2, 2, 16, C), BF), pltpu.SemaphoreType.DMA((4,))]
    return pl.pallas_call(
        functools.partial(filter_kernel, side),
        out_shape=tuple(outs),
        in_specs=[IN_VMEM] * (len(operands) - 1) + [IN_HBM],
        out_specs=[IN_VMEM] * len(outs),
        scratch_shapes=scratch,
        compiler_params=params(8),
        cost_estimate=cost(1e8, 1e5),
        name="filter_part",
    )(*operands[:-1], in_hbm(operands[-1]))


def edge_kernel(left_ref, right_ref, total_ref, near_ref, far_ref, _, __, own_ref, other_ref, chip_cot_ref, link_cot_ref, sems):
    core = lax.axis_index("core")
    copies = []
    for ref, first in ((chip_cot_ref, 2 - 2 * core), (link_cot_ref, 2 * core)):
        for source, start in ((left_ref, 0), (right_ref, EDGE + NJ)):
            target = ref.at[:, pl.ds(start, EDGE)]
            copies.append(pltpu.make_async_copy(source.at[pl.ds(first, 2)], target, sems.at[len(copies)]))
    for copy in copies:
        copy.start()
    edges = []
    for side in range(2):
        for row in range(2):
            i = 2 - 2 * row_pair(side) + row
            edges += [right_ref[i], left_ref[i]]
    edges = jnp.concatenate(edges, axis=0).T
    for k in range(K):
        columns = slice(k * C, (k + 1) * C)
        beyond = jnp.concatenate([near_ref[2 * NJ :, columns], far_ref[2 * NJ :, columns]], axis=0)
        total = total_ref[:, columns] + jnp.dot(edges, beyond, preferred_element_type=F32)
        first, second = total[:LANES], total[LANES:]
        mine = jnp.where(core == 0, first, second)
        theirs = jnp.where(core == 0, second, first).astype(BF)
        for part in range(2):
            lanes = slice(part * LANES, (part + 1) * LANES)
            own_ref[2 * k + part] = mine[:, lanes]
            other_ref[2 * k + part] = theirs[:, lanes]
    for block in range(BLOCKS, PADDED_BLOCKS):
        own_ref[block] = jnp.zeros((LANES, LANES), F32)
        other_ref[block] = jnp.zeros((LANES, LANES), BF)
    for copy in copies:
        copy.wait()


def edge_part(left, right, total, near, far, chip_cot, link_cot):
    shape = (PADDED_BLOCKS, LANES, LANES)
    return pl.pallas_call(
        edge_kernel,
        out_shape=(
            pltpu.VMEM(shape, F32),
            pltpu.VMEM(shape, BF),
            pltpu.VMEM((2, WIDE, C), BF),
            pltpu.VMEM((2, WIDE, C), BF),
        ),
        in_specs=[IN_VMEM] * 5 + [ANYWHERE] * 2,
        out_specs=[IN_VMEM] * 2 + [ANYWHERE] * 2,
        input_output_aliases={5: 2, 6: 3},
        scratch_shapes=[pltpu.SemaphoreType.DMA((4,))],
        compiler_params=params(4),
        cost_estimate=cost(1e9, 4e6),
        name="edge_part",
    )(left, right, total, near, far, chip_cot, link_cot)


def half_kernel(own_ref, other_ref, _, out_ref, half, sems):
    copies = []
    for n in range(4):
        part = pl.ds(n * PADDED_BLOCKS // 4, PADDED_BLOCKS // 4)
        half[part] = (own_ref[part] + other_ref[part].astype(F32)).astype(BF)
        copies.append(pltpu.make_async_copy(half.at[part], out_ref.at[part], sems.at[n]))
        copies[n].start()
    for copy in copies:
        copy.wait()


def half_part(own, other, after):
    return pl.pallas_call(
        half_kernel,
        out_shape=jax.ShapeDtypeStruct(own.shape, BF),
        in_specs=[IN_VMEM] * 2 + [ANYWHERE],
        out_specs=IN_HBM,
        scratch_shapes=[pltpu.VMEM(own.shape, BF), pltpu.SemaphoreType.DMA((4,))],
        compiler_params=params(4),
        cost_estimate=cost(1e6, 3e6),
        name="half_part",
    )(own, other, after)


def mixed_kernel(side, filtered_ref, weight_ref, *refs):
    mixed_ref, ends_ref, to_right_ref, to_left_ref = refs[-4:]
    place = 2 * side
    if side == 1:
        to_right_ref[0:2] = refs[0][...]
        to_left_ref[0:2] = refs[1][...]
    beyond = jnp.dot(filtered_ref[2 * NJ :, :], weight_ref[...], preferred_element_type=F32)
    for row in range(2):
        to_right_ref[place + row] = beyond[row * J : row * J + EDGE]
        to_left_ref[place + row] = beyond[row * J + EDGE : (row + 1) * J]
        found = jnp.dot(
            filtered_ref[row * NJ : (row + 1) * NJ, :], weight_ref[...], preferred_element_type=F32
        )
        ends_ref[row, 0:EDGE, :] = found[0:EDGE]
        ends_ref[row, EDGE:, :] = found[NJ - EDGE :]
        mixed_ref[row] = found.astype(BF)


def mixed_part(side, *operands):
    return pl.pallas_call(
        functools.partial(mixed_kernel, side),
        out_shape=(
            pltpu.VMEM((2, NJ, C), BF),
            pltpu.VMEM((2, 2 * EDGE, C), F32),
            pltpu.VMEM((2 + 2 * side, EDGE, C), F32),
            pltpu.VMEM((2 + 2 * side, EDGE, C), F32),
        ),
        in_specs=[IN_VMEM] * len(operands),
        out_specs=[IN_VMEM] * 4,
        compiler_params=params(4),
        cost_estimate=cost(1e8, 1e5),
        name="mixed_part",
    )(*operands)


def ends_kernel(near_ends_ref, far_ends_ref, left_ref, right_ref, near_ref, far_ref, _, out_ref, done_ref, ends, sems):
    middle = pl.ds(EDGE, NJ - 2 * EDGE)
    copies = []
    for side, (ends_ref, mixed_ref) in enumerate(((near_ends_ref, near_ref), (far_ends_ref, far_ref))):
        rows = pl.ds(2 - 2 * row_pair(side), 2)
        places = slice(2 * side, 2 * side + 2)
        copies.append(pltpu.make_async_copy(mixed_ref.at[:, middle], out_ref.at[rows, middle], sems.at[side, 2]))
        copies[-1].start()
        ends[side, 0] = (ends_ref[:, 0:EDGE, :] + left_ref[places]).astype(BF)
        ends[side, 1] = (ends_ref[:, EDGE:, :] + right_ref[places]).astype(BF)
        for n, first in enumerate((0, NJ - EDGE)):
            target = out_ref.at[rows, pl.ds(first, EDGE)]
            copies.append(pltpu.make_async_copy(ends.at[side, n], target, sems.at[side, n]))
            copies[-1].start()
    done_ref[...] = jnp.zeros_like(done_ref)
    for copy in copies:
        copy.wait()


def ends_part(near_ends, far_ends, left, right, near, far, after):
    return pl.pallas_call(
        ends_kernel,
        out_shape=(jax.ShapeDtypeStruct((ROWS, NJ, C), BF), pltpu.VMEM((8, LANES), F32)),
        in_specs=[IN_VMEM] * 6 + [ANYWHERE],
        out_specs=[IN_HBM, IN_VMEM],
        scratch_shapes=[pltpu.VMEM((2, 2, 2, EDGE, C), BF), pltpu.SemaphoreType.DMA((2, 3))],
        compiler_params=params(4),
        cost_estimate=cost(1e6, 1e6),
        name="ends_part",
    )(near_ends, far_ends, left, right, near, far, after)


def sum_kernel(scale, pieces_ref, out_ref):
    piece = (jnp.sum(pieces_ref[...].astype(F32), axis=0) * scale).astype(BF)
    out_ref[...] = jnp.broadcast_to(piece, out_ref.shape)


def sum_part(pieces, scale):
    return pl.pallas_call(
        functools.partial(sum_kernel, scale),
        out_shape=pltpu.VMEM(pieces.shape, BF),
        in_specs=[IN_VMEM],
        out_specs=IN_VMEM,
        compiler_params=params(4),
        cost_estimate=cost(1e6, 2e6),
        name="sum_part",
    )(pieces)


def order_kernel(*_):
    pass


def ordered(value, after):
    return pl.pallas_call(
        order_kernel,
        out_shape=jax.ShapeDtypeStruct(value.shape, value.dtype),
        in_specs=[ANYWHERE, ANYWHERE],
        out_specs=ANYWHERE,
        input_output_aliases={0: 0},
        compiler_params=params(1),
        name="ordered",
    )(value, after)


def result_kernel(side, half_ref, *refs):
    out_ref, block, sems = refs[-3:]
    core = lax.axis_index("core")
    lanes = pl.ds(pl.multiple_of((core if side == 0 else 1 - core) * LANES, LANES), LANES)
    copies = []
    for k in range(K):
        for part in range(2):
            block[k, part * LANES : (part + 1) * LANES, :] = half_ref[2 * k + part].astype(F32).T
        copies.append(pltpu.make_async_copy(block.at[k], out_ref.at[k, :, lanes], sems.at[k]))
        copies[k].start()
    for copy in copies:
        copy.wait()


def result_part(half, result=None):
    given = [] if result is None else [result]
    return pl.pallas_call(
        functools.partial(result_kernel, len(given)),
        out_shape=jax.ShapeDtypeStruct((K, C, C), F32),
        in_specs=[IN_VMEM] + [IN_HBM] * len(given),
        out_specs=IN_HBM,
        input_output_aliases={1: 0} if given else {},
        scratch_shapes=[pltpu.VMEM((K, C, LANES), F32), pltpu.SemaphoreType.DMA((K,))],
        compiler_params=params(6),
        cost_estimate=cost(1e6, 4e6),
        name="result_part",
    )(half, *given)


def extend(extended, n, row, left, right):
    extended[n] = jnp.concatenate([left, row, right], axis=0)


def grad_kernel(kept_ref, chip_ref, link_ref, left_ref, right_ref, weight_hbm, cot_hbm, _, out_ref, done_ref, weight, weight_turned, cot, extended, bands, cells, filtered, mixed, sems):
    core = lax.axis_index("core")
    cot_copy = pltpu.make_async_copy(cot_hbm, cot, sems.at[ROWS])
    cot_copy.start()
    weight_copy = pltpu.make_async_copy(weight_hbm, weight, sems.at[ROWS + 1])
    weight_copy.start()

    def fill(low, high):
        for n in range(2):
            extended[n] = low[n, 8 : 8 + EXT, :]
            extended[6 + n] = high[n, 8 : 8 + EXT, :]
            cells[n] = low[n, 2 * EDGE + NJ :, 0:LANES]
            cells[6 + n] = high[n, 2 * EDGE + NJ :, 0:LANES]

    pl.when(core == 0)(lambda: fill(link_ref, chip_ref))
    pl.when(core == 1)(lambda: fill(chip_ref, link_ref))
    for n in range(ROWS):
        cells[2 + n] = kept_ref[n]

    away = (TAPS - 1 - lax.broadcasted_iota(jnp.int32, (16, LANES), 1)) // WIDTH
    place = one_hot(lambda tap: (TAPS - 1 - tap) // WIDTH * EXT_WINDOW + 8 - RAD + (TAPS - 1 - tap) % WIDTH)
    lines = []
    for row in range(ROWS):
        taken = jnp.zeros((16, LANES), F32)
        for r in range(WIDTH):
            taken = jnp.where(away == r, cells[row + r].astype(F32), taken)
        lines.append(jnp.dot(taken.astype(BF), place, preferred_element_type=F32))
    cot_copy.wait()
    for n in range(ROWS):
        extend(extended, 2 + n, cot[n], left_ref[n, 8:, :], right_ref[n, :8, :])
    copies = [pltpu.make_async_copy(mixed.at[row], out_ref.at[row], sems.at[row]) for row in range(ROWS)]
    for row in range(ROWS):
        slot = row % 2
        for k in range(K):
            bands[slot, k * J : (k + 1) * J, :] = banded(lines[row][k : k + 1, :])[:, :DEPTH]
        for tile in range(STEPS):
            start = tile * J
            window = jnp.concatenate(
                [extended[row + r, start : start + EXT_WINDOW, :] for r in range(WIDTH)], axis=0
            )
            found = jnp.dot(bands[slot], window, preferred_element_type=F32).astype(BF)
            for k in range(K):
                filtered[slot, start : start + J, k * C : (k + 1) * C] = found[k * J : (k + 1) * J]
        if row == 0:
            weight_copy.wait()
            for k in range(K):
                columns = slice(k * C, (k + 1) * C)
                weight_turned[columns, :] = weight[columns, :].T
        mixed[row] = jnp.dot(filtered[slot], weight_turned[...], preferred_element_type=F32).astype(BF)
        copies[row].start()
    for copy in copies:
        copy.wait()
    done_ref[...] = jnp.zeros_like(done_ref)


def grad_part(kept, chip, link, left, right, weight, cotangent, after):
    return pl.pallas_call(
        grad_kernel,
        out_shape=(jax.ShapeDtypeStruct((ROWS, NJ, C), BF), pltpu.VMEM((8, LANES), F32)),
        in_specs=[IN_VMEM] * 5 + [IN_HBM, IN_HBM, ANYWHERE],
        out_specs=[IN_HBM, IN_VMEM],
        scratch_shapes=[
            pltpu.VMEM((K * C, C), BF),
            pltpu.VMEM((K * C, C), BF),
            pltpu.VMEM((ROWS, NJ, C), BF),
            pltpu.VMEM((PLACES, EXT, C), BF),
            pltpu.VMEM((2, K * J, DEPTH), BF),
            pltpu.VMEM((PLACES, 16, LANES), BF),
            pltpu.VMEM((2, NJ, K * C), BF),
            pltpu.VMEM((ROWS, NJ, C), BF),
            pltpu.SemaphoreType.DMA((ROWS + 2,)),
        ],
        compiler_params=params(20),
        cost_estimate=cost(8e9, 5e6),
        name="grad_input_part",
    )(kept, chip, link, left, right, in_hbm(weight), in_hbm(cotangent), after)


def shifted(block, axis, count, step, periodic):
    route = [(i, (i + step) % count) for i in range(count) if periodic or 0 <= i + step < count]
    return lax.ppermute(block, axis, route)


def per_device(features, basis, span_lo, span_hi, weight, cotangent):
    lat, chips = ("yz", "core"), ("yz", "lon")
    lats, lons = lax.axis_size("yz") * lax.axis_size("core"), lax.axis_size("lon")
    parts = lax.axis_size("yz") * lons
    swap = [(0, 1), (1, 0)]

    pairs = [(i, i + 1) for i in range(1, lats - 1, 2)]
    pairs = pairs + [(b, a) for a, b in pairs]
    sent_chip, sent_link = send_part(features)
    weight = weight.reshape(K * C, C)
    to_right, to_left, kept, bands = own_part(
        span_lo, span_hi, basis, cotangent, sent_link
    )
    chip = lax.ppermute(sent_chip, "core", swap)
    link = lax.ppermute(sent_link, lat, pairs)
    near_left = shifted(to_right, "lon", lons, 1, True)
    near_right = shifted(to_left, "lon", lons, -1, True)
    total, near, weight_near = filter_part(0, chip, sent_chip, sent_link, bands, cotangent, weight)
    near_mixed, near_ends, to_right, to_left = mixed_part(0, near, weight_near)
    total, far, chip_cot, link_cot = filter_part(
        1, link, sent_chip, sent_link, bands, cotangent, total, kept, to_right, cotangent
    )
    own, other, chip_cot, link_cot = edge_part(near_left, near_right, total, near, far, chip_cot, link_cot)

    other = lax.ppermute(other, "core", swap)
    far_mixed, far_ends, to_right, to_left = mixed_part(1, far, weight_near, to_right, to_left)
    half = half_part(own, other, far_ends)
    pieces = lax.all_to_all(half.reshape(parts, -1, LANES), chips, 0, 0)
    link_cot = lax.ppermute(ordered(link_cot, half), lat, pairs)
    chip_cot = lax.ppermute(ordered(chip_cot, half), "core", swap)
    left = shifted(ordered(to_right, half), "lon", lons, 1, True)
    right = shifted(ordered(to_left, half), "lon", lons, -1, True)
    scale = 1.0 / math.sqrt(ROWS * lats * NJ * lons)
    copies = sum_part(pieces, scale)
    gathered = lax.all_to_all(copies, chips, 0, 0).reshape(PADDED_BLOCKS, LANES, LANES)
    mixed, mixed_done = ends_part(near_ends, far_ends, left, right, near_mixed, far_mixed, copies)
    grad_input, grad_done = grad_part(
        kept, chip_cot, link_cot, near_left, near_right, weight, cotangent, mixed_done
    )
    gathered = ordered(gathered, grad_done)
    other = lax.ppermute(gathered, "core", swap)
    grad_weight = result_part(other, result_part(gathered))
    return mixed, grad_input, grad_weight


def solution(mesh):
    lats, lons = mesh.devices.shape
    split = Mesh(mesh.devices.reshape(lats // 2, 2, lons), ("yz", "core", "lon"))
    lat = ("yz", "core")
    return jax.shard_map(
        per_device,
        mesh=split,
        in_specs=(P(lat, "lon", None), P(lat, None, None), P(lat), P(lat), P(), P(lat, "lon", None)),
        out_specs=(P(lat, "lon", None), P(lat, "lon", None), P()),
        check_vma=False,
    )
```
